32 devices in a mesh: mode: 2 (over y), space: 16 (over z, x, core).
Axes of the slice: x: 2, y: 2, z: 4, core: 2. Of those that a mesh axis runs over, the one named last changes fastest.
Arguments:
- solution: bfloat16 [64, 32, 32, 256], P('mode', 'space'), may hold values from -6 to 6
- source: bfloat16 [64, 32, 32, 256], P('mode', 'space'), may hold values from -12 to 12
- conductivity: bfloat16 [16, 32, 32, 256], P('mode', 'space'), may hold values from -1.5 to 4, as said below
- triples: int32 [4096, 4], replicated, may hold values from -8 to 63, as said below
Outputs:
- updated: float32 [64, 32, 32, 256], P('mode', 'space')
The draws below stay inside these ranges and needn't reach their ends.
Inputs may be any that keep to these rules, and one draw needn't show every extreme that they name: Mode 0 of conductivity lies in 0.5 to 4 at every cell; modes 1 to 15 are signed. `triples`: columns hold i and j in 0 to 63, k in 0 to 15, and an integer weight in -8 to 16, never 0. The rows (i, i, 0, 16) appear for every i, and with every other row (i, j, k, w) the row (j, i, k, w) appears too; k is 1 or more in those.
All inputs are finite; a program needn't handle non-finite values.
Results may differ from the reference program's by a relative error of at most 0.0003.
Values may be sent and summed in bfloat16 or wider, within the bound.
No kernel may reach another device: no remote copies, remote signals or barrier semaphores. Data moves between devices by JAX's collectives and lax.ppermute only.
A program may use at most 128 MiB of HBM per device.

```python
import jax
import jax.numpy as jnp
from jax import lax

P_SIZE = 64
K = 16
PAIRS = 2016
NY = 32
NZ = 256
NX = 32


def draw_conductivity(key, part):
    key = jax.random.fold_in(key, 2)
    key_mean, key_rest = jax.random.split(key)
    mean_field = jnp.exp(jax.random.uniform(key_mean, (1, NX, NY, NZ), jnp.float32, jnp.log(0.5), jnp.log(4.0)))
    rest_field = 0.5 * jnp.clip(jax.random.normal(key_rest, (K - 1, NX, NY, NZ), jnp.float32), -3.0, 3.0)
    return jnp.concatenate([mean_field, rest_field], axis=0).astype(jnp.bfloat16)


def draw_triples(key, part):
    key = jax.random.fold_in(key, 1)
    key_rows, key_cols, key_modes, key_sizes, key_signs = jax.random.split(key, 5)
    diag_index = jnp.arange(P_SIZE, dtype=jnp.int32)
    identity_rows = jnp.stack([diag_index, diag_index, jnp.zeros((P_SIZE,), jnp.int32), jnp.full((P_SIZE,), 16, jnp.int32)], axis=1)
    first = jax.random.randint(key_rows, (PAIRS,), 0, P_SIZE, jnp.int32)
    second = jax.random.randint(key_cols, (PAIRS,), 0, P_SIZE, jnp.int32)
    modes = jax.random.randint(key_modes, (PAIRS,), 1, K, jnp.int32)
    magnitude = jax.random.randint(key_sizes, (PAIRS,), 1, 9, jnp.int32)
    signs = jax.random.randint(key_signs, (PAIRS,), 0, 2, jnp.int32) * 2 - 1
    weights = magnitude * signs
    forward = jnp.stack([first, second, modes, weights], axis=1)
    backward = jnp.stack([second, first, modes, weights], axis=1)
    return jnp.concatenate([identity_rows, forward, backward], axis=0)


def levels(stream_key, shape, pieces, low, largest):
    def one(position, blocks):
        steps = jax.random.uniform(jax.random.fold_in(jax.random.fold_in(stream_key, 6), position), (blocks,), jnp.float32, low / len(pieces), largest / len(pieces))
        return jnp.repeat(jnp.exp(steps), shape[position] // blocks).reshape((-1,) + (1,) * (len(shape) - position - 1))

    factor_of = one(*pieces[0])
    for cut in pieces[1:]:
        factor_of = factor_of * one(*cut)
    return factor_of


def noise(key, shape, spread, reach, pieces=(), held_as=jnp.bfloat16):
    drawn = spread * jax.random.normal(key, shape, jnp.float32)
    if pieces:
        drawn = drawn * levels(key, shape, pieces, -0.22, 0.18)
    return jnp.clip(drawn, -reach, reach).astype(held_as)


def setup_inputs(seed: int = 0) -> dict:
    streams_of = jax.random.split(jax.random.key(seed), 5)
    return {
        "solution": noise(streams_of[0], (P_SIZE, NX, NY, NZ), 1.0, 6.0, ((0, 2), (1, 16))),
        "source": noise(streams_of[1], (P_SIZE, NX, NY, NZ), 2.0, 12.0, ((0, 2), (1, 16))),
        "conductivity": draw_conductivity(jax.random.fold_in(streams_of[4], 71), 0),
        "triples": draw_triples(jax.random.fold_in(streams_of[4], 71), 0),
    }


weight_scale = 16.0
relax_factor = 2.0 / 3.0


def coupling_matrices(triples):
    rows = triples[:, 0]
    columns = triples[:, 1]
    modes = triples[:, 2]
    weights = triples[:, 3].astype(jnp.float32) / weight_scale
    dense = jnp.zeros((K, P_SIZE, P_SIZE), jnp.float32).at[modes, rows, columns].add(weights)
    return dense.astype(jnp.bfloat16)


def shifted(array, offset_x, offset_y, offset_z):
    size_x, size_y, size_z = array.shape[-3], array.shape[-2], array.shape[-1]
    return array[..., 1 + offset_x:size_x - 1 + offset_x, 1 + offset_y:size_y - 1 + offset_y, 1 + offset_z:size_z - 1 + offset_z]


neighbour_offsets = ((1, 0, 0), (-1, 0, 0), (0, 1, 0), (0, -1, 0), (0, 0, 1), (0, 0, -1))


def stencil_core(field_padded, cond_padded):
    centre_field = shifted(field_padded, 0, 0, 0)
    centre_cond = shifted(cond_padded, 0, 0, 0)
    result = jnp.zeros(centre_field.shape, jnp.float32)
    for offsets in neighbour_offsets:
        conduct = 0.5 * (centre_cond + shifted(cond_padded, *offsets))
        result = result + conduct * (centre_field - shifted(field_padded, *offsets))
    return result


def diagonal_core(cond_padded):
    centre_cond = shifted(cond_padded, 0, 0, 0)
    result = jnp.zeros(centre_cond.shape, jnp.float32)
    for offsets in neighbour_offsets:
        result = result + 0.5 * (centre_cond + shifted(cond_padded, *offsets))
    return result


def reference(solution, source, conductivity, triples):
    coupling = coupling_matrices(triples)
    cond_padded = jnp.pad(conductivity.astype(jnp.float32), ((0, 0), (1, 1), (1, 1), (1, 1)))
    flat = solution.reshape(P_SIZE, -1)

    def one_mode(summed, inputs):
        matrix, cond_one = inputs
        mixed = jnp.dot(matrix, flat, preferred_element_type=jnp.float32).reshape(solution.shape)
        mixed_padded = jnp.pad(mixed, ((0, 0), (1, 1), (1, 1), (1, 1)))
        return summed + stencil_core(mixed_padded, cond_one), None

    applied, unused = lax.scan(one_mode, jnp.zeros(solution.shape, jnp.float32), (coupling, cond_padded))
    diagonal = diagonal_core(cond_padded[0])
    return solution.astype(jnp.float32) + relax_factor * (source.astype(jnp.float32) - applied) / diagonal
```

```python
import functools

import jax
import jax.numpy as jnp
from jax import lax
from jax.experimental import pallas as pl
from jax.experimental.pallas import tpu as pltpu
from jax.sharding import PartitionSpec as P

CHUNKS = 4
LANES = 128
VMEM = 56 * 2**20

weight_scale = 16.0
relax_factor = 2.0 / 3.0


def neighbours_of(axis):
    count = lax.axis_size(axis)
    forward = [(i, i + 1) for i in range(count - 1)]
    return forward, [(target, source) for source, target in forward]


def from_others(block):
    count = lax.axis_size("mode")
    return [
        lax.ppermute(block, "mode", [((i + step) % count, i) for i in range(count)])
        for step in range(1, count)
    ]


def coupling_rows(triples, cond_count, all_modes, local_modes, cond_local):
    me = lax.axis_index("mode")
    row = triples[:, 0] - me * local_modes
    column = (triples[:, 1] - me * local_modes) % all_modes
    mode = (triples[:, 2] - me * cond_local) % cond_count
    inside = (row >= 0) & (row < local_modes)
    code = jnp.where(inside, mode * local_modes + row, -1)
    entries = triples.shape[0]
    left = code[None, :] == lax.broadcasted_iota(
        jnp.int32, (cond_count * local_modes, entries), 0
    )
    right = jnp.where(
        column[:, None] == lax.broadcasted_iota(jnp.int32, (entries, all_modes), 1),
        triples[:, 3].astype(jnp.bfloat16)[:, None],
        jnp.bfloat16(0),
    )
    summed = jnp.dot(left.astype(jnp.bfloat16), right, preferred_element_type=jnp.float32)
    coupling = (summed / weight_scale).astype(jnp.bfloat16)
    half = coupling * jnp.bfloat16(0.5)
    return jnp.concatenate([half] + [-half] * 4, axis=1)


def apply_kernel(row0, cond_count, local_modes, first, matrix, own, other, cond_all, total, face_low, face_high, edge_low, edge_high, scale, field, summed, band, cond, weights, mixed, around, sem):
    planes, rows, size_z = total.shape[0], total.shape[1], total.shape[3]
    all_modes = field.shape[2]
    window = pltpu.make_async_copy(cond_all.at[:, row0 : row0 + rows + 2], cond, sem)
    window.start()
    blank = jnp.zeros((planes, all_modes, size_z), jnp.bfloat16)
    field[:, 0] = blank
    field[:, rows + 1] = blank
    field[:, 1 : rows + 1, :local_modes, :] = own[...]
    field[:, 1 : rows + 1, local_modes:, :] = other[...]
    to = lax.broadcasted_iota(jnp.int32, (size_z, size_z), 0)
    at = lax.broadcasted_iota(jnp.int32, (size_z, size_z), 1)
    band[...] = jnp.where(jnp.abs(to - at) == 1, 1.0, 0.0).astype(jnp.bfloat16)
    for x in range(planes):
        for y in range(rows):
            value = jnp.dot(field[x, y + 1], band[...], preferred_element_type=jnp.float32)
            for side in (x - 1, x + 1):
                if 0 <= side < planes:
                    value = value + field[side, y + 1].astype(jnp.float32)
            coarse = value.astype(jnp.bfloat16)
            summed[x, y, :all_modes] = coarse
            summed[x, y, all_modes:] = (value - coarse.astype(jnp.float32)).astype(jnp.bfloat16)
    window.wait()
    lane = lax.broadcasted_iota(jnp.int32, (cond_count, size_z), 1)
    lane_out = lax.broadcasted_iota(jnp.int32, (local_modes, size_z), 1)

    def both_sides(value, lanes):
        above = jnp.where(lanes == size_z - 1, 0.0, pltpu.roll(value, size_z - 1, 1))
        below = jnp.where(lanes == 0, 0.0, pltpu.roll(value, 1, 1))
        return above + below

    def mix(x, y):
        mixed[x] = jnp.dot(matrix[:, :all_modes], field[x, y + 1], preferred_element_type=jnp.float32)
        nearby = jnp.concatenate([summed[x, y], field[x, y], field[x, y + 2]], axis=0)
        around[x] = jnp.dot(matrix[:, all_modes:], nearby, preferred_element_type=jnp.float32)

    def conduct(x, y):
        def row(i, j):
            return cond[i, j].astype(jnp.float32)

        centre = row(x + 1, y + 1)
        low, high = row(x, y + 1), row(x + 2, y + 1)
        weights[x, 0] = centre
        weights[x, 1] = (
            6.0 * centre + (low + high) + (row(x + 1, y) + row(x + 1, y + 2)) + both_sides(centre, lane)
        )
        if x == 0:
            weights[x, 2] = centre + low
        if x == planes - 1:
            weights[x, 2 + (planes == 1)] = centre + high

    def sums(x):
        outer = [2] if x in (0, planes - 1) else []
        if planes == 1:
            outer = [2, 3]
        halves = []
        for start in range(0, size_z, LANES):
            part = slice(start, start + LANES)
            accs = [None] * (2 + len(outer))

            def add(which, term):
                accs[which] = term if accs[which] is None else accs[which] + term

            for k in range(cond_count):
                here = slice(k * local_modes, (k + 1) * local_modes)
                value = mixed[x, here, part]

                def weight(d):
                    return jnp.broadcast_to(weights[x, d, pl.ds(k, 1), part], value.shape)

                centre = weight(0)
                add(0, weight(1) * value)
                add(0, centre * around[x, here, part])
                add(1, centre * value)
                for n, d in enumerate(outer):
                    add(2 + n, weight(d) * value)
            halves.append(accs)
        return [jnp.concatenate([h[d] for h in halves], axis=1) for d in range(len(halves[0]))]

    def edge_sums(x, y, side):
        terms = None
        for k in range(cond_count):
            weight = (cond[x + 1, y + 1].astype(jnp.float32) + cond[x + 1, side].astype(jnp.float32))[k : k + 1]
            term = weight * mixed[x, k * local_modes : (k + 1) * local_modes, :]
            terms = term if terms is None else terms + term
        return terms

    for x in range(planes):
        mix(x, 0)

    def one_row(y, carry):
        later = jnp.minimum(y + 1, rows - 1)
        products = []
        for x in range(planes):
            conduct(x, y)
            scale[x, pl.ds(y, 1), :] = (2.0 * relax_factor) / weights[x, 1, pl.ds(first[0], 1), :]

            @pl.when(y == 0)
            def _():
                edge_low[x] = edge_sums(x, 0, 0)

            @pl.when(y == rows - 1)
            def _():
                edge_high[x] = edge_sums(x, rows - 1, rows + 1)

            found = sums(x)
            mix(x, later)
            if x == 0:
                face_low[y] = found[2]
            if x == planes - 1:
                face_high[y] = found[2 + (planes == 1)]
            products.append(found[1])
            total[x, y] = found[0] - both_sides(found[1], lane_out) - carry[x]

            @pl.when(y > 0)
            def _():
                total[x, y - 1] = total[x, y - 1] - found[1]

        for x in range(planes):
            for side in (x - 1, x + 1):
                if 0 <= side < planes:
                    total[x, y] = total[x, y] - products[side]
        return tuple(products)

    zero = jnp.zeros((local_modes, size_z), jnp.float32)
    lax.fori_loop(0, rows, one_row, (zero,) * planes)


def finish_kernel(total, from_low, from_high, before, after, own, source, scale, done, result, *parts):
    del done
    planes, rows = total.shape[0], total.shape[1]
    modes = total.shape[2]
    size_z = total.shape[3]
    for x in range(planes):
        for y in range(rows):
            applied = total[x, y]
            if x == 0:
                applied = applied - from_low[y]
            if x == planes - 1:
                applied = applied - from_high[y]
            if y == 0:
                applied = applied - before[x]
            if y == rows - 1:
                applied = applied - after[x]
            value = own[x, y].astype(jnp.float32) + (
                source[x, y].astype(jnp.float32) - applied
            ) * scale[x, y : y + 1, :]
            for part, flat in enumerate(parts):
                flat[pl.ds(x * rows + y, modes, planes * rows), :] = value[
                    :, part * LANES : (part + 1) * LANES
                ]
    for part, flat in enumerate(parts):
        result[:, :, :, part * LANES : (part + 1) * LANES] = flat[...].reshape(
            modes, planes, rows, LANES
        )


def shards(solution, source, conductivity, triples):
    mode_count = lax.axis_size("mode")
    local_modes, planes, size_y, size_z = solution.shape
    all_modes = local_modes * mode_count
    cond_local = conductivity.shape[0]
    cond_count = cond_local * mode_count
    forward, backward = neighbours_of("space")
    step = size_y // CHUNKS

    cond_own = jnp.transpose(conductivity, (1, 2, 0, 3))
    cond_all = jnp.concatenate([cond_own] + from_others(cond_own), axis=2)
    owns = [
        jnp.transpose(solution[:, :, c * step : (c + 1) * step], (1, 2, 0, 3)) for c in range(CHUNKS)
    ]
    others = [jnp.concatenate(from_others(own), axis=2) for own in owns]
    cond_low = lax.ppermute(cond_all[planes - 1 :], "space", forward)
    cond_high = lax.ppermute(cond_all[:1], "space", backward)
    cond = jnp.concatenate([cond_low, cond_all, cond_high], axis=0)
    cond = jnp.pad(cond, ((0, 0), (1, 1), (0, 0), (0, 0)))
    matrix = coupling_rows(triples, cond_count, all_modes, local_modes, cond_local)
    source_rows = jnp.transpose(source, (1, 2, 0, 3))

    first = ((cond_count - lax.axis_index("mode") * cond_local) % cond_count).reshape(1)
    whole = pl.BlockSpec(memory_space=pltpu.VMEM)
    params = pltpu.CompilerParams(vmem_limit_bytes=VMEM)
    rows_shape = jax.ShapeDtypeStruct((step, local_modes, size_z), jnp.float32)
    edge_shape = jax.ShapeDtypeStruct((planes, local_modes, size_z), jnp.float32)
    parts = []
    for c in range(CHUNKS):
        total, low, high, edge_low, edge_high, scale = pl.pallas_call(
            functools.partial(apply_kernel, c * step, cond_count, local_modes),
            out_shape=(
                jax.ShapeDtypeStruct((planes, step, local_modes, size_z), jnp.float32),
                rows_shape,
                rows_shape,
                edge_shape,
                edge_shape,
                jax.ShapeDtypeStruct((planes, step, size_z), jnp.float32),
            ),
            in_specs=[pl.BlockSpec(memory_space=pltpu.SMEM)]
            + [whole] * 3
            + [pl.BlockSpec(memory_space=pl.ANY)],
            out_specs=(whole,) * 6,
            scratch_shapes=[
                pltpu.VMEM((planes, step + 2, all_modes, size_z), jnp.bfloat16),
                pltpu.VMEM((planes, step, 2 * all_modes, size_z), jnp.bfloat16),
                pltpu.VMEM((size_z, size_z), jnp.bfloat16),
                pltpu.VMEM((planes + 2, step + 2, cond_count, size_z), jnp.bfloat16),
                pltpu.VMEM((planes, 4, cond_count, size_z), jnp.float32),
                pltpu.VMEM((planes, cond_count * local_modes, size_z), jnp.float32),
                pltpu.VMEM((planes, cond_count * local_modes, size_z), jnp.float32),
                pltpu.SemaphoreType.DMA,
            ],
            compiler_params=params,
        )(first, matrix, owns[c], others[c], cond)
        from_low = lax.ppermute(high, "space", forward)
        from_high = lax.ppermute(low, "space", backward)
        parts.append((total, from_low, from_high, edge_low, edge_high, scale))

    nothing = jnp.zeros((planes, local_modes, size_z), jnp.float32)
    result = None
    for c, (total, from_low, from_high, edge_low, edge_high, scale) in enumerate(parts):
        before = parts[c - 1][4] if c else nothing
        after = parts[c + 1][3] if c + 1 < CHUNKS else nothing
        args = [total, from_low, from_high, before, after, owns[c], source_rows, scale]

        def at(i, c=c):
            return (0, c, 0, 0)

        specs = [whole] * len(args)
        specs[6] = pl.BlockSpec((planes, step, local_modes, size_z), at)
        result_in = jnp.zeros((1,), jnp.float32) if result is None else result
        alias = {} if result is None else {len(args): 0}
        result = pl.pallas_call(
            finish_kernel,
            grid=(1,),
            out_shape=jax.ShapeDtypeStruct((local_modes, planes, size_y, size_z), jnp.float32),
            in_specs=specs + [pl.BlockSpec(memory_space=pl.ANY)],
            out_specs=pl.BlockSpec((local_modes, planes, step, size_z), lambda i, c=c: (0, 0, c, 0)),
            scratch_shapes=[pltpu.VMEM((local_modes * planes * step, LANES), jnp.float32)]
            * (size_z // LANES),
            input_output_aliases=alias,
            compiler_params=params,
        )(*args, result_in)
    return result


def solution(mesh):
    return jax.shard_map(
        shards,
        mesh=mesh,
        in_specs=(
            P("mode", "space", None, None),
            P("mode", "space", None, None),
            P("mode", "space", None, None),
            P(),
        ),
        out_specs=P("mode", "space", None, None),
        check_vma=False,
    )
```

```python
import functools

import jax
import jax.numpy as jnp
from jax import lax
from jax.experimental import pallas as pl
from jax.experimental.pallas import tpu as pltpu
from jax.sharding import PartitionSpec as P

CHUNKS = 4
SLOTS = 4
LANES = 128
VMEM = 20 * 2**20

weight_scale = 16.0
relax_factor = 2.0 / 3.0


def neighbours_of(axis):
    count = lax.axis_size(axis)
    forward = [(i, i + 1) for i in range(count - 1)]
    return forward, [(target, source) for source, target in forward]


def from_others(block):
    count = lax.axis_size("mode")
    return [
        lax.ppermute(block, "mode", [((i + step) % count, i) for i in range(count)])
        for step in range(1, count)
    ]


def coupling_rows(triples, cond_count, all_modes, local_modes, cond_local):
    me = lax.axis_index("mode")
    row = triples[:, 0] - me * local_modes
    column = (triples[:, 1] - me * local_modes) % all_modes
    mode = (triples[:, 2] - me * cond_local) % cond_count
    inside = (row >= 0) & (row < local_modes)
    code = jnp.where(inside, mode * local_modes + row, -1)
    entries = triples.shape[0]
    left = code[None, :] == lax.broadcasted_iota(
        jnp.int32, (cond_count * local_modes, entries), 0
    )
    right = jnp.where(
        column[:, None] == lax.broadcasted_iota(jnp.int32, (entries, all_modes), 1),
        triples[:, 3].astype(jnp.bfloat16)[:, None],
        jnp.bfloat16(0),
    )
    summed = jnp.dot(left.astype(jnp.bfloat16), right, preferred_element_type=jnp.float32)
    coupling = (summed / weight_scale).astype(jnp.bfloat16)
    half = coupling * jnp.bfloat16(0.5)
    return jnp.concatenate([half] + [-half] * 4, axis=1)


def apply_kernel(row0, cond_count, local_modes, first, matrix, own, other, cond_all, total, face_low, face_high, edge_low, edge_high, scale, field, summed, band, cond, plain, weights, mixed, around, product, sem):
    planes, rows, size_z = total.shape[0], total.shape[1], total.shape[3]
    all_modes = field.shape[2]
    slots = mixed.shape[0]
    steps = [(y, x) for y in range(rows) for x in range(planes)]
    window = pltpu.make_async_copy(cond_all.at[:, row0 : row0 + rows + 2], cond, sem)
    window.start()
    blank = jnp.zeros((planes, all_modes, size_z), jnp.bfloat16)
    field[:, 0] = blank
    field[:, rows + 1] = blank
    field[:, 1 : rows + 1, :local_modes, :] = own[...]
    field[:, 1 : rows + 1, local_modes:, :] = other[...]
    to = lax.broadcasted_iota(jnp.int32, (size_z, size_z), 0)
    at = lax.broadcasted_iota(jnp.int32, (size_z, size_z), 1)
    band[...] = jnp.where(jnp.abs(to - at) == 1, 1.0, 0.0).astype(jnp.bfloat16)
    window.wait()
    plain[...] = cond[...].astype(jnp.float32)
    lane = lax.broadcasted_iota(jnp.int32, (cond_count, size_z), 1)
    lane_out = lax.broadcasted_iota(jnp.int32, (local_modes, size_z), 1)

    def both_sides(value, lanes):
        above = jnp.where(lanes == size_z - 1, 0.0, pltpu.roll(value, size_z - 1, 1))
        below = jnp.where(lanes == 0, 0.0, pltpu.roll(value, 1, 1))
        return above + below

    def nearby_sum(y, x):
        value = jnp.dot(field[x, y + 1], band[...], preferred_element_type=jnp.float32)
        for side in (x - 1, x + 1):
            if 0 <= side < planes:
                value = value + field[side, y + 1].astype(jnp.float32)
        coarse = value.astype(jnp.bfloat16)
        summed[x, y, :all_modes] = coarse
        summed[x, y, all_modes:] = (value - coarse.astype(jnp.float32)).astype(jnp.bfloat16)

    def mix(step):
        y, x = steps[step]
        slot = step % slots
        mixed[slot] = jnp.dot(matrix[:, :all_modes], field[x, y + 1], preferred_element_type=jnp.float32)
        nearby = jnp.concatenate([summed[x, y], field[x, y], field[x, y + 2]], axis=0)
        around[slot] = jnp.dot(matrix[:, all_modes:], nearby, preferred_element_type=jnp.float32)

    def sums(step):
        y, x = steps[step]
        slot = step % slots
        centre = plain[x + 1, y + 1]
        low, high = plain[x, y + 1], plain[x + 2, y + 1]
        front, back = plain[x + 1, y], plain[x + 1, y + 2]
        weights[slot, 0] = 6.0 * centre + ((low + high) + (front + back)) + both_sides(centre, lane)
        outer = []
        if x == 0:
            outer.append((low, face_low, y))
        if x == planes - 1:
            outer.append((high, face_high, y))
        if y == 0:
            outer.append((front, edge_low, x))
        if y == rows - 1:
            outer.append((back, edge_high, x))
        for n, (side, _, _) in enumerate(outer):
            weights[slot, 1 + n] = centre + side
        scale[x, y : y + 1, :] = (2.0 * relax_factor) / weights[slot, 0, pl.ds(first[0], 1), :]
        for start in range(0, size_z, LANES):
            part = slice(start, start + LANES)
            accs = [None] * (2 + len(outer))

            def add(which, term):
                accs[which] = term if accs[which] is None else accs[which] + term

            for k in range(cond_count):
                here = slice(k * local_modes, (k + 1) * local_modes)
                value = mixed[slot, here, part]
                middle = jnp.broadcast_to(plain[x + 1, y + 1, k : k + 1, part], value.shape)
                add(1, middle * value)
                add(0, middle * around[slot, here, part])
                for n in range(1 + len(outer)):
                    weight = jnp.broadcast_to(weights[slot, n, k : k + 1, part], value.shape)
                    add(n + (n > 0), weight * value)
            total[x, y, :, part] = accs[0]
            product[x, y, :, part] = accs[1]
            for n, (_, target, index) in enumerate(outer):
                target[index, :, part] = accs[2 + n]

    def close(y):
        for x in range(planes):
            value = total[x, y] - both_sides(product[x, y], lane_out)
            for side in (x - 1, x + 1):
                if 0 <= side < planes:
                    value = value - product[side, y]
            for side in (y - 1, y + 1):
                if 0 <= side < rows:
                    value = value - product[x, side]
            total[x, y] = value

    ahead = slots - 1
    for step in range(len(steps)):
        nearby_sum(*steps[step])
    for step in range(ahead):
        mix(step)
    for step in range(len(steps)):
        if step + ahead < len(steps):
            mix(step + ahead)
        sums(step)
        y, x = steps[step]
        if x == planes - 1 and y > 0:
            close(y - 1)
    close(rows - 1)


def finish_kernel(total, from_low, from_high, before, after, own, source, scale, done, result, *parts):
    del done
    planes, rows = total.shape[0], total.shape[1]
    modes = total.shape[2]
    size_z = total.shape[3]
    for x in range(planes):
        for y in range(rows):
            applied = total[x, y]
            if x == 0:
                applied = applied - from_low[y]
            if x == planes - 1:
                applied = applied - from_high[y]
            if y == 0:
                applied = applied - before[x]
            if y == rows - 1:
                applied = applied - after[x]
            value = own[x, y].astype(jnp.float32) + (
                source[x, y].astype(jnp.float32) - applied
            ) * scale[x, y : y + 1, :]
            for part, flat in enumerate(parts):
                flat[pl.ds(x * rows + y, modes, planes * rows), :] = value[
                    :, part * LANES : (part + 1) * LANES
                ]
    for part, flat in enumerate(parts):
        result[:, :, :, part * LANES : (part + 1) * LANES] = flat[...].reshape(
            modes, planes, rows, LANES
        )


def shards(solution, source, conductivity, triples):
    mode_count = lax.axis_size("mode")
    local_modes, planes, size_y, size_z = solution.shape
    all_modes = local_modes * mode_count
    cond_local = conductivity.shape[0]
    cond_count = cond_local * mode_count
    forward, backward = neighbours_of("space")
    step = size_y // CHUNKS

    cond_own = jnp.transpose(conductivity, (1, 2, 0, 3))
    cond_all = jnp.concatenate([cond_own] + from_others(cond_own), axis=2)
    owns = [
        jnp.transpose(solution[:, :, c * step : (c + 1) * step], (1, 2, 0, 3)) for c in range(CHUNKS)
    ]
    others = [jnp.concatenate(from_others(own), axis=2) for own in owns]
    cond_low = lax.ppermute(cond_all[planes - 1 :], "space", forward)
    cond_high = lax.ppermute(cond_all[:1], "space", backward)
    cond = jnp.concatenate([cond_low, cond_all, cond_high], axis=0)
    cond = jnp.pad(cond, ((0, 0), (1, 1), (0, 0), (0, 0)))
    matrix = coupling_rows(triples, cond_count, all_modes, local_modes, cond_local)
    source_rows = jnp.transpose(source, (1, 2, 0, 3))

    first = ((cond_count - lax.axis_index("mode") * cond_local) % cond_count).reshape(1)
    whole = pl.BlockSpec(memory_space=pltpu.VMEM)
    params = pltpu.CompilerParams(vmem_limit_bytes=VMEM)
    rows_shape = jax.ShapeDtypeStruct((step, local_modes, size_z), jnp.float32)
    edge_shape = jax.ShapeDtypeStruct((planes, local_modes, size_z), jnp.float32)
    parts = []
    for c in range(CHUNKS):
        total, low, high, edge_low, edge_high, scale = pl.pallas_call(
            functools.partial(apply_kernel, c * step, cond_count, local_modes),
            out_shape=(
                jax.ShapeDtypeStruct((planes, step, local_modes, size_z), jnp.float32),
                rows_shape,
                rows_shape,
                edge_shape,
                edge_shape,
                jax.ShapeDtypeStruct((planes, step, size_z), jnp.float32),
            ),
            in_specs=[pl.BlockSpec(memory_space=pltpu.SMEM)]
            + [whole] * 3
            + [pl.BlockSpec(memory_space=pl.ANY)],
            out_specs=(whole,) * 6,
            scratch_shapes=[
                pltpu.VMEM((planes, step + 2, all_modes, size_z), jnp.bfloat16),
                pltpu.VMEM((planes, step, 2 * all_modes, size_z), jnp.bfloat16),
                pltpu.VMEM((size_z, size_z), jnp.bfloat16),
                pltpu.VMEM((planes + 2, step + 2, cond_count, size_z), jnp.bfloat16),
                pltpu.VMEM((planes + 2, step + 2, cond_count, size_z), jnp.float32),
                pltpu.VMEM((SLOTS, 4, cond_count, size_z), jnp.float32),
                pltpu.VMEM((SLOTS, cond_count * local_modes, size_z), jnp.float32),
                pltpu.VMEM((SLOTS, cond_count * local_modes, size_z), jnp.float32),
                pltpu.VMEM((planes, step, local_modes, size_z), jnp.float32),
                pltpu.SemaphoreType.DMA,
            ],
            compiler_params=params,
        )(first, matrix, owns[c], others[c], cond)
        from_low = lax.ppermute(high, "space", forward)
        from_high = lax.ppermute(low, "space", backward)
        parts.append((total, from_low, from_high, edge_low, edge_high, scale))

    nothing = jnp.zeros((planes, local_modes, size_z), jnp.float32)
    result = None
    for c, (total, from_low, from_high, edge_low, edge_high, scale) in enumerate(parts):
        before = parts[c - 1][4] if c else nothing
        after = parts[c + 1][3] if c + 1 < CHUNKS else nothing
        args = [total, from_low, from_high, before, after, owns[c], source_rows, scale]

        def at(i, c=c):
            return (0, c, 0, 0)

        specs = [whole] * len(args)
        specs[6] = pl.BlockSpec((planes, step, local_modes, size_z), at)
        result_in = jnp.zeros((1,), jnp.float32) if result is None else result
        alias = {} if result is None else {len(args): 0}
        result = pl.pallas_call(
            finish_kernel,
            grid=(1,),
            out_shape=jax.ShapeDtypeStruct((local_modes, planes, size_y, size_z), jnp.float32),
            in_specs=specs + [pl.BlockSpec(memory_space=pl.ANY)],
            out_specs=pl.BlockSpec((local_modes, planes, step, size_z), lambda i, c=c: (0, 0, c, 0)),
            scratch_shapes=[pltpu.VMEM((local_modes * planes * step, LANES), jnp.float32)]
            * (size_z // LANES),
            input_output_aliases=alias,
            compiler_params=params,
        )(*args, result_in)
    return result


def solution(mesh):
    return jax.shard_map(
        shards,
        mesh=mesh,
        in_specs=(
            P("mode", "space", None, None),
            P("mode", "space", None, None),
            P("mode", "space", None, None),
            P(),
        ),
        out_specs=P("mode", "space", None, None),
        check_vma=False,
    )
```

```python
import functools

import jax
import jax.numpy as jnp
from jax import lax
from jax.experimental import pallas as pl
from jax.experimental.pallas import tpu as pltpu
from jax.sharding import PartitionSpec as P

CHUNKS = 4
SLOTS = 4
LANES = 128
VMEM = 20 * 2**20

weight_scale = 16.0
relax_factor = 2.0 / 3.0


def pairings(axis):
    count = lax.axis_size(axis)
    found = []
    for start in (0, 1):
        pairs = [(i, i + 1) for i in range(start, count - 1, 2)]
        found.append(pairs + [(high, low) for low, high in pairs])
    return found


def from_others(block):
    count = lax.axis_size("mode")
    return [
        lax.ppermute(block, "mode", [((i + step) % count, i) for i in range(count)])
        for step in range(1, count)
    ]


def coupling_rows(triples, cond_count, all_modes, local_modes, cond_local):
    me = lax.axis_index("mode")
    row = triples[:, 0] - me * local_modes
    column = (triples[:, 1] - me * local_modes) % all_modes
    mode = (triples[:, 2] - me * cond_local) % cond_count
    inside = (row >= 0) & (row < local_modes)
    code = jnp.where(inside, mode * local_modes + row, -1)
    entries = triples.shape[0]
    left = code[None, :] == lax.broadcasted_iota(
        jnp.int32, (cond_count * local_modes, entries), 0
    )
    right = jnp.where(
        column[:, None] == lax.broadcasted_iota(jnp.int32, (entries, all_modes), 1),
        triples[:, 3].astype(jnp.bfloat16)[:, None],
        jnp.bfloat16(0),
    )
    summed = jnp.dot(left.astype(jnp.bfloat16), right, preferred_element_type=jnp.float32)
    coupling = (summed / weight_scale).astype(jnp.bfloat16)
    half = coupling * jnp.bfloat16(0.5)
    return jnp.concatenate([half] + [-half] * 4, axis=1)


def apply_kernel(row0, cond_count, local_modes, with_faces, info, matrix, own, other, cond_all, total, edge_low, edge_high, scale, *rest):
    if with_faces:
        first_face, second_face, *rest, faces = rest
    field, summed, band, cond, plain, weights, mixed, around, product, sem = rest
    planes, rows, size_z = total.shape[0], total.shape[1], total.shape[3]
    parity = info[1]
    all_modes = field.shape[2]
    slots = mixed.shape[0]
    steps = [(y, x) for y in range(rows) for x in range(planes)]
    window = pltpu.make_async_copy(cond_all.at[:, row0 : row0 + rows + 2], cond, sem)
    window.start()
    blank = jnp.zeros((planes, all_modes, size_z), jnp.bfloat16)
    field[:, 0] = blank
    field[:, rows + 1] = blank
    field[:, 1 : rows + 1, :local_modes, :] = own[...]
    field[:, 1 : rows + 1, local_modes:, :] = other[...]
    to = lax.broadcasted_iota(jnp.int32, (size_z, size_z), 0)
    at = lax.broadcasted_iota(jnp.int32, (size_z, size_z), 1)
    band[...] = jnp.where(jnp.abs(to - at) == 1, 1.0, 0.0).astype(jnp.bfloat16)
    window.wait()
    plain[...] = cond[...].astype(jnp.float32)
    lane = lax.broadcasted_iota(jnp.int32, (cond_count, size_z), 1)
    lane_out = lax.broadcasted_iota(jnp.int32, (local_modes, size_z), 1)

    def both_sides(value, lanes):
        above = jnp.where(lanes == size_z - 1, 0.0, pltpu.roll(value, size_z - 1, 1))
        below = jnp.where(lanes == 0, 0.0, pltpu.roll(value, 1, 1))
        return above + below

    def nearby_sum(y, x):
        value = jnp.dot(field[x, y + 1], band[...], preferred_element_type=jnp.float32)
        for side in (x - 1, x + 1):
            if 0 <= side < planes:
                value = value + field[side, y + 1].astype(jnp.float32)
        coarse = value.astype(jnp.bfloat16)
        summed[x, y, :all_modes] = coarse
        summed[x, y, all_modes:] = (value - coarse.astype(jnp.float32)).astype(jnp.bfloat16)

    def mix(step):
        y, x = steps[step]
        slot = step % slots
        mixed[slot] = jnp.dot(matrix[:, :all_modes], field[x, y + 1], preferred_element_type=jnp.float32)
        nearby = jnp.concatenate([summed[x, y], field[x, y], field[x, y + 2]], axis=0)
        around[slot] = jnp.dot(matrix[:, all_modes:], nearby, preferred_element_type=jnp.float32)

    def sums(step):
        y, x = steps[step]
        slot = step % slots
        centre = plain[x + 1, y + 1]
        low, high = plain[x, y + 1], plain[x + 2, y + 1]
        front, back = plain[x + 1, y], plain[x + 1, y + 2]
        weights[slot, 0] = 6.0 * centre + ((low + high) + (front + back)) + both_sides(centre, lane)
        outer = []
        if with_faces and x == 0:
            outer.append((low, faces, (1 - parity, y)))
        if with_faces and x == planes - 1:
            outer.append((high, faces, (parity, y)))
        if y == 0:
            outer.append((front, edge_low, (x,)))
        if y == rows - 1:
            outer.append((back, edge_high, (x,)))
        for n, (side, _, _) in enumerate(outer):
            weights[slot, 1 + n] = centre + side
        scale[x, y : y + 1, :] = (2.0 * relax_factor) / weights[slot, 0, pl.ds(info[0], 1), :]
        for start in range(0, size_z, LANES):
            part = slice(start, start + LANES)
            accs = [None] * (2 + len(outer))

            def add(which, term):
                accs[which] = term if accs[which] is None else accs[which] + term

            for k in range(cond_count):
                here = slice(k * local_modes, (k + 1) * local_modes)
                value = mixed[slot, here, part]
                middle = jnp.broadcast_to(plain[x + 1, y + 1, k : k + 1, part], value.shape)
                add(1, middle * value)
                add(0, middle * around[slot, here, part])
                for n in range(1 + len(outer)):
                    weight = jnp.broadcast_to(weights[slot, n, k : k + 1, part], value.shape)
                    add(n + (n > 0), weight * value)
            total[x, y, :, part] = accs[0]
            product[x, y, :, part] = accs[1]
            for n, (_, target, index) in enumerate(outer):
                target[(*index, slice(None), part)] = accs[2 + n]

    def close(y):
        for x in range(planes):
            value = total[x, y] - both_sides(product[x, y], lane_out)
            for side in (x - 1, x + 1):
                if 0 <= side < planes:
                    value = value - product[side, y]
            for side in (y - 1, y + 1):
                if 0 <= side < rows:
                    value = value - product[x, side]
            total[x, y] = value

    ahead = slots - 1
    for step in range(len(steps)):
        nearby_sum(*steps[step])
    for step in range(ahead):
        mix(step)
    for step in range(len(steps)):
        if step + ahead < len(steps):
            mix(step + ahead)
        sums(step)
        y, x = steps[step]
        if x == planes - 1 and y > 0:
            close(y - 1)
    close(rows - 1)
    if with_faces:
        first_face[...] = faces[0]
        second_face[...] = faces[1]


def face_kernel(row0, cond_count, local_modes, info, matrix, own, other, cond_all, first_face, second_face, field, cond, weights, mixed, faces, sem):
    planes, rows, size_z = own.shape[0], own.shape[1], own.shape[3]
    parity = info[1]
    slots = mixed.shape[0]
    steps = [(y, x, side) for y in range(rows) for x, side in ((0, 0), (planes - 1, planes + 1))]
    window = pltpu.make_async_copy(cond_all.at[:, row0 + 1 : row0 + rows + 1], cond, sem)
    window.start()
    field[:, :, :local_modes, :] = own[...]
    field[:, :, local_modes:, :] = other[...]
    window.wait()

    def mix(step):
        y, x, _ = steps[step]
        mixed[step % slots] = jnp.dot(
            matrix[:, : field.shape[2]], field[x, y], preferred_element_type=jnp.float32
        )

    for step in range(slots - 1):
        mix(step)
    for step, (y, x, side) in enumerate(steps):
        if step + slots - 1 < len(steps):
            mix(step + slots - 1)
        slot = step % slots
        weights[slot] = cond[x + 1, y].astype(jnp.float32) + cond[side, y].astype(jnp.float32)
        for start in range(0, size_z, LANES):
            part = slice(start, start + LANES)
            acc = None
            for k in range(cond_count):
                value = mixed[slot, k * local_modes : (k + 1) * local_modes, part]
                term = jnp.broadcast_to(weights[slot, k : k + 1, part], value.shape) * value
                acc = term if acc is None else acc + term
            faces[1 - parity if side == 0 else parity, y, :, part] = acc
    first_face[...] = faces[0]
    second_face[...] = faces[1]


def finish_kernel(info, total, from_first, from_second, before, after, own, source, scale, done, result, *parts):
    del done
    planes, rows = total.shape[0], total.shape[1]
    modes = total.shape[2]
    size_z = total.shape[3]
    for x in range(planes):
        for y in range(rows):
            applied = total[x, y]
            if x == 0:
                applied = applied - jnp.where(info[1] == 0, from_second[y], from_first[y])
            if x == planes - 1:
                applied = applied - jnp.where(info[1] == 0, from_first[y], from_second[y])
            if y == 0:
                applied = applied - before[x]
            if y == rows - 1:
                applied = applied - after[x]
            value = own[x, y].astype(jnp.float32) + (
                source[x, y].astype(jnp.float32) - applied
            ) * scale[x, y : y + 1, :]
            for part, flat in enumerate(parts):
                flat[pl.ds(x * rows + y, modes, planes * rows), :] = value[
                    :, part * LANES : (part + 1) * LANES
                ]
    for part, flat in enumerate(parts):
        result[:, :, :, part * LANES : (part + 1) * LANES] = flat[...].reshape(
            modes, planes, rows, LANES
        )


def shards(solution, source, conductivity, triples):
    mode_count = lax.axis_size("mode")
    local_modes, planes, size_y, size_z = solution.shape
    all_modes = local_modes * mode_count
    cond_local = conductivity.shape[0]
    cond_count = cond_local * mode_count
    first_pairs, second_pairs = pairings("space")
    step = size_y // CHUNKS
    parity = lax.axis_index("space") % 2
    even = parity == 0

    def swap(for_first, for_second):
        return (
            lax.ppermute(for_first, "space", first_pairs),
            lax.ppermute(for_second, "space", second_pairs),
        )

    cond_others = from_others(conductivity)
    sent = [
        jnp.transpose(solution[:, :, c * step : (c + 1) * step], (1, 2, 0, 3)) for c in range(CHUNKS)
    ]
    owns, others, arrived = [], [], [cond_others[0]] if cond_others else []
    for c in range(CHUNKS):
        own = sent[c]
        if 1 <= c < len(arrived) + 1:
            own, _ = lax.optimization_barrier((own, arrived[c - 1]))
        pieces = from_others(own)
        owns.append(own)
        others.append(jnp.concatenate(pieces, axis=2))
        arrived.append(pieces[0])

    cond_all = jnp.transpose(jnp.concatenate([conductivity] + cond_others, axis=0), (1, 2, 0, 3))
    top, bottom = cond_all[planes - 1 :], cond_all[:1]
    cond_first, cond_second = swap(jnp.where(even, top, bottom), jnp.where(even, bottom, top))
    cond_low = jnp.where(even, cond_second, cond_first)
    cond_high = jnp.where(even, cond_first, cond_second)
    cond = jnp.concatenate([cond_low, cond_all, cond_high], axis=0)
    cond = jnp.pad(cond, ((0, 0), (1, 1), (0, 0), (0, 0)))
    matrix = coupling_rows(triples, cond_count, all_modes, local_modes, cond_local)
    source_rows = jnp.transpose(source, (1, 2, 0, 3))
    first = (cond_count - lax.axis_index("mode") * cond_local) % cond_count
    info = jnp.stack([first, parity]).astype(jnp.int32)

    whole = pl.BlockSpec(memory_space=pltpu.VMEM)
    scalars = pl.BlockSpec(memory_space=pltpu.SMEM)
    params = pltpu.CompilerParams(vmem_limit_bytes=VMEM)
    rows_shape = jax.ShapeDtypeStruct((step, local_modes, size_z), jnp.float32)
    edge_shape = jax.ShapeDtypeStruct((planes, local_modes, size_z), jnp.float32)
    faces_scratch = pltpu.VMEM((2, step, local_modes, size_z), jnp.float32)
    mixed_scratch = pltpu.VMEM((SLOTS, cond_count * local_modes, size_z), jnp.float32)
    inputs = [scalars] + [whole] * 3 + [pl.BlockSpec(memory_space=pl.ANY)]
    parts = []
    for c in range(CHUNKS):
        last = c == CHUNKS - 1
        args = (info, matrix, owns[c], others[c], cond)
        if last:
            faces = pl.pallas_call(
                functools.partial(face_kernel, c * step, cond_count, local_modes),
                out_shape=(rows_shape,) * 2,
                in_specs=inputs,
                out_specs=(whole,) * 2,
                scratch_shapes=[
                    pltpu.VMEM((planes, step, all_modes, size_z), jnp.bfloat16),
                    pltpu.VMEM((planes + 2, step, cond_count, size_z), jnp.bfloat16),
                    pltpu.VMEM((SLOTS, cond_count, size_z), jnp.float32),
                    mixed_scratch,
                    faces_scratch,
                    pltpu.SemaphoreType.DMA,
                ],
                compiler_params=params,
            )(*args)
            from_first, from_second = swap(*faces)
        total, edge_low, edge_high, scale, *faces = pl.pallas_call(
            functools.partial(apply_kernel, c * step, cond_count, local_modes, not last),
            out_shape=(
                jax.ShapeDtypeStruct((planes, step, local_modes, size_z), jnp.float32),
                edge_shape,
                edge_shape,
                jax.ShapeDtypeStruct((planes, step, size_z), jnp.float32),
            )
            + (rows_shape,) * (0 if last else 2),
            in_specs=inputs,
            out_specs=(whole,) * (4 if last else 6),
            scratch_shapes=[
                pltpu.VMEM((planes, step + 2, all_modes, size_z), jnp.bfloat16),
                pltpu.VMEM((planes, step, 2 * all_modes, size_z), jnp.bfloat16),
                pltpu.VMEM((size_z, size_z), jnp.bfloat16),
                pltpu.VMEM((planes + 2, step + 2, cond_count, size_z), jnp.bfloat16),
                pltpu.VMEM((planes + 2, step + 2, cond_count, size_z), jnp.float32),
                pltpu.VMEM((SLOTS, 4, cond_count, size_z), jnp.float32),
                mixed_scratch,
                mixed_scratch,
                pltpu.VMEM((planes, step, local_modes, size_z), jnp.float32),
                pltpu.SemaphoreType.DMA,
            ]
            + ([] if last else [faces_scratch]),
            compiler_params=params,
        )(*args)
        if not last:
            from_first, from_second = swap(*faces)
        parts.append((total, from_first, from_second, edge_low, edge_high, scale))

    nothing = jnp.zeros((planes, local_modes, size_z), jnp.float32)
    result = None
    for c, (total, from_first, from_second, edge_low, edge_high, scale) in enumerate(parts):
        before = parts[c - 1][4] if c else nothing
        after = parts[c + 1][3] if c + 1 < CHUNKS else nothing
        args = [info, total, from_first, from_second, before, after, owns[c], source_rows, scale]

        def at(i, c=c):
            return (0, c, 0, 0)

        specs = [scalars] + [whole] * (len(args) - 1)
        specs[7] = pl.BlockSpec((planes, step, local_modes, size_z), at)
        result_in = jnp.zeros((1,), jnp.float32) if result is None else result
        alias = {} if result is None else {len(args): 0}
        result = pl.pallas_call(
            finish_kernel,
            grid=(1,),
            out_shape=jax.ShapeDtypeStruct((local_modes, planes, size_y, size_z), jnp.float32),
            in_specs=specs + [pl.BlockSpec(memory_space=pl.ANY)],
            out_specs=pl.BlockSpec((local_modes, planes, step, size_z), lambda i, c=c: (0, 0, c, 0)),
            scratch_shapes=[pltpu.VMEM((local_modes * planes * step, LANES), jnp.float32)]
            * (size_z // LANES),
            input_output_aliases=alias,
            compiler_params=params,
        )(*args, result_in)
    return result


def solution(mesh):
    return jax.shard_map(
        shards,
        mesh=mesh,
        in_specs=(
            P("mode", "space", None, None),
            P("mode", "space", None, None),
            P("mode", "space", None, None),
            P(),
        ),
        out_specs=P("mode", "space", None, None),
        check_vma=False,
    )
```

```python
import functools

import jax
import jax.numpy as jnp
from jax import lax
from jax.experimental import pallas as pl
from jax.experimental.pallas import tpu as pltpu
from jax.sharding import PartitionSpec as P

UNITS = (2, 3, 3)
BAND = 8
SLOTS = 4
PARTS = 4
LANES = 128
VMEM = 18 * 2**20

weight_scale = 16.0
relax_factor = 2.0 / 3.0


def pairings(axis):
    count = lax.axis_size(axis)
    found = []
    for start in (0, 1):
        pairs = [(i, i + 1) for i in range(start, count - 1, 2)]
        found.append(pairs + [(high, low) for low, high in pairs])
    return found


def from_others(block):
    count = lax.axis_size("mode")
    return [
        lax.ppermute(block, "mode", [((i + step) % count, i) for i in range(count)])
        for step in range(1, count)
    ]


def coupling_kernel(cond_count, all_modes, local_modes, info, triples, matrix):
    inner = PARTS if cond_count % PARTS == 0 else 1
    entries = triples.shape[1]
    width = min(entries, 512)
    total = jnp.zeros((cond_count // inner * local_modes, inner * all_modes), jnp.float32)
    for start in range(0, entries, width):
        here = slice(start, start + width)
        row = triples[0:1, here] - info[2]
        column = triples[1:2, here] - info[2]
        column = jnp.where(column < 0, column + all_modes, column)
        mode = triples[2:3, here] - info[3]
        mode = jnp.where(mode < 0, mode + cond_count, mode)
        weight = triples[3:4, here].astype(jnp.float32)
        upper = mode // inner
        inside = (row >= 0) & (row < local_modes)
        left_code = jnp.where(inside, upper * local_modes + row, -1)
        right_code = (mode - upper * inner) * all_modes + column
        left = jnp.where(
            left_code == lax.broadcasted_iota(jnp.int32, (total.shape[0], width), 0), weight, 0.0
        )
        right = jnp.where(
            right_code == lax.broadcasted_iota(jnp.int32, (total.shape[1], width), 0), 1.0, 0.0
        )
        total = total + lax.dot_general(
            left.astype(jnp.bfloat16),
            right.astype(jnp.bfloat16),
            (((1,), (1,)), ((), ())),
            preferred_element_type=jnp.float32,
        )
    coupling = (total / weight_scale).astype(jnp.bfloat16).astype(jnp.float32) * 0.5
    for mode in range(cond_count):
        upper, lower = divmod(mode, inner)
        block = coupling[
            upper * local_modes : (upper + 1) * local_modes, lower * all_modes : (lower + 1) * all_modes
        ]
        wide = jnp.concatenate([block] + [-block] * 4, axis=1)
        matrix[mode * local_modes : (mode + 1) * local_modes, :] = wide.astype(jnp.bfloat16)


def apply_kernel(row0, cond_count, local_modes, info, matrix, own, other, cond_all, total, face, edge_low, edge_high, scale, field, summed, band, cond, plain, weights, mixed, around, product, sem):
    planes, rows, size_z = total.shape[0], total.shape[1], total.shape[3]
    all_modes = field.shape[2]
    slots = mixed.shape[0]
    steps = [(y, x) for y in range(rows) for x in range(planes)]
    window = pltpu.make_async_copy(cond_all.at[:, row0 : row0 + rows + 2], cond, sem)
    window.start()
    blank = jnp.zeros((planes, all_modes, size_z), jnp.bfloat16)
    field[:, 0] = blank
    field[:, rows + 1] = blank
    field[:, 1 : rows + 1, :local_modes, :] = own[...]
    field[:, 1 : rows + 1, local_modes:, :] = other[...]
    to = lax.broadcasted_iota(jnp.int32, (size_z, size_z), 0)
    at = lax.broadcasted_iota(jnp.int32, (size_z, size_z), 1)
    band[...] = jnp.where(jnp.abs(to - at) == 1, 1.0, 0.0).astype(jnp.bfloat16)
    window.wait()
    plain[...] = cond[...].astype(jnp.float32)
    lane = lax.broadcasted_iota(jnp.int32, (cond_count, size_z), 1)
    lane_out = lax.broadcasted_iota(jnp.int32, (local_modes, size_z), 1)

    def both_sides(value, lanes):
        above = jnp.where(lanes == size_z - 1, 0.0, pltpu.roll(value, size_z - 1, 1))
        below = jnp.where(lanes == 0, 0.0, pltpu.roll(value, 1, 1))
        return above + below

    def nearby_sum(y, x):
        value = jnp.dot(field[x, y + 1], band[...], preferred_element_type=jnp.float32)
        for side in (x - 1, x + 1):
            if 0 <= side < planes:
                value = value + field[side, y + 1].astype(jnp.float32)
        coarse = value.astype(jnp.bfloat16)
        summed[x, y, :all_modes] = coarse
        summed[x, y, all_modes:] = (value - coarse.astype(jnp.float32)).astype(jnp.bfloat16)

    def mix(step):
        y, x = steps[step]
        slot = step % slots
        mixed[slot] = jnp.dot(matrix[:, :all_modes], field[x, y + 1], preferred_element_type=jnp.float32)
        nearby = jnp.concatenate([summed[x, y], field[x, y], field[x, y + 2]], axis=0)
        around[slot] = jnp.dot(matrix[:, all_modes:], nearby, preferred_element_type=jnp.float32)

    def sums(step):
        y, x = steps[step]
        slot = step % slots
        centre = plain[x + 1, y + 1]
        low, high = plain[x, y + 1], plain[x + 2, y + 1]
        front, back = plain[x + 1, y], plain[x + 1, y + 2]
        weights[slot, 0] = 6.0 * centre + ((low + high) + (front + back)) + both_sides(centre, lane)
        outer = []
        if x == planes - 1:
            outer.append((high, face, (y,)))
        if y == 0:
            outer.append((front, edge_low, (x,)))
        if y == rows - 1:
            outer.append((back, edge_high, (x,)))
        for n, (side, _, _) in enumerate(outer):
            weights[slot, 1 + n] = centre + side
        scale[x, y : y + 1, :] = (2.0 * relax_factor) / weights[slot, 0, pl.ds(info[0], 1), :]
        for start in range(0, size_z, LANES):
            part = slice(start, start + LANES)
            accs = [None] * (2 + len(outer))

            def add(which, term):
                accs[which] = term if accs[which] is None else accs[which] + term

            for k in range(cond_count):
                here = slice(k * local_modes, (k + 1) * local_modes)
                value = mixed[slot, here, part]
                middle = jnp.broadcast_to(plain[x + 1, y + 1, k : k + 1, part], value.shape)
                add(1, middle * value)
                add(0, middle * around[slot, here, part])
                for n in range(1 + len(outer)):
                    weight = jnp.broadcast_to(weights[slot, n, k : k + 1, part], value.shape)
                    add(n + (n > 0), weight * value)
            total[x, y, :, part] = accs[0]
            product[x, y, :, part] = accs[1]
            for n, (_, target, index) in enumerate(outer):
                target[(*index, slice(None), part)] = accs[2 + n]

    def close(y):
        for x in range(planes):
            value = total[x, y] - both_sides(product[x, y], lane_out)
            for side in (x - 1, x + 1):
                if 0 <= side < planes:
                    value = value - product[side, y]
            for side in (y - 1, y + 1):
                if 0 <= side < rows:
                    value = value - product[x, side]
            total[x, y] = value

    ahead = slots - 1
    for step in range(len(steps)):
        nearby_sum(*steps[step])
    for step in range(ahead):
        mix(step)
    for step in range(len(steps)):
        if step + ahead < len(steps):
            mix(step + ahead)
        sums(step)
        y, x = steps[step]
        if x == planes - 1 and y > 0:
            close(y - 1)
    close(rows - 1)


def finish_kernel(steps, cond_count, local_modes, info, matrix, cond, from_first, halo_own, halo_early, halo_late, source, *rest):
    chunks = len(steps)
    per_chunk = [rest[5 * c : 5 * c + 5] for c in range(chunks)]
    result, weights, mixed, sem = rest[5 * chunks], *rest[5 * chunks + 1 : 5 * chunks + 4]
    planes, _, modes, size_z = per_chunk[0][0].shape
    halves = size_z // LANES
    stages = [rest[5 * chunks + 4 + slot * halves :][:halves] for slot in range(2)]
    slots = mixed.shape[0]
    parity = info[1]
    places = [(c, y) for c in range(chunks) for y in range(steps[c])]
    total_rows = len(places)
    all_modes = matrix.shape[1] // 5
    pieces = all_modes // local_modes - 1

    def mix(row):
        c, y = places[row]
        beyond = [halo_own[row]]
        for piece in range(pieces):
            if c < 2:
                beyond.append(halo_early[pieces * sum(steps[:c]) + piece * steps[c] + y])
            else:
                beyond.append(halo_late[piece * steps[c] + y])
        mixed[row % slots] = jnp.dot(
            matrix[:, :all_modes], jnp.concatenate(beyond, axis=0), preferred_element_type=jnp.float32
        )

    def beyond_face(row):
        slot = row % slots
        weights[slot] = cond[0, row + 1].astype(jnp.float32) + cond[1, row + 1].astype(jnp.float32)
        out = []
        for start in range(0, size_z, LANES):
            part = slice(start, start + LANES)
            acc = None
            for k in range(cond_count):
                value = mixed[slot, k * local_modes : (k + 1) * local_modes, part]
                term = jnp.broadcast_to(weights[slot, k : k + 1, part], value.shape) * value
                acc = term if acc is None else acc + term
            out.append(acc)
        return jnp.concatenate(out, axis=1)

    for row in range(slots - 1):
        mix(row)
    copies = []
    for band in range(total_rows // BAND):
        stage = stages[band % 2]
        if band >= 2:
            for copy in copies[band - 2]:
                copy.wait()
        for line in range(BAND):
            row = band * BAND + line
            if row + slots - 1 < total_rows:
                mix(row + slots - 1)
            c, y = places[row]
            total, _, _, scale, own = per_chunk[c]
            for x in range(planes):
                natural = x + parity * (planes - 1 - 2 * x)
                applied = total[x, y]
                if x == 0:
                    applied = applied - beyond_face(row)
                if x == planes - 1:
                    applied = applied - from_first[row]
                if y == 0 and c > 0:
                    applied = applied - per_chunk[c - 1][2][x]
                if y == steps[c] - 1 and c < chunks - 1:
                    applied = applied - per_chunk[c + 1][1][x]
                value = own[x, y].astype(jnp.float32) + (
                    source[natural, row].astype(jnp.float32) - applied
                ) * scale[x, y : y + 1, :]
                for h in range(halves):
                    flat = stage[h].reshape(modes * planes * BAND, LANES)
                    flat[pl.ds(natural * BAND + line, modes, planes * BAND), :] = value[
                        :, h * LANES : (h + 1) * LANES
                    ]
        copies.append(
            [
                pltpu.make_async_copy(
                    stage[h],
                    result.at[:, :, band * BAND : (band + 1) * BAND, h * LANES : (h + 1) * LANES],
                    sem.at[band % 2, h],
                )
                for h in range(halves)
            ]
        )
        for copy in copies[band]:
            copy.start()
    for waiting in copies[-2:]:
        for copy in waiting:
            copy.wait()


def shards(solution, source, conductivity, triples):
    mode_count = lax.axis_size("mode")
    local_modes, planes, size_y, size_z = solution.shape
    all_modes = local_modes * mode_count
    cond_local = conductivity.shape[0]
    cond_count = cond_local * mode_count
    first_pairs, second_pairs = pairings("space")
    unit = size_y // sum(UNITS)
    chunks = len(UNITS)
    starts = [unit * sum(UNITS[:c]) for c in range(chunks)]
    steps = [unit * units for units in UNITS]
    parity = lax.axis_index("space") % 2

    def oriented(block):
        return jnp.where(parity == 0, block, jnp.flip(block, 1))

    cond_own = oriented(conductivity)
    own_rows = lax.optimization_barrier(jnp.transpose(oriented(solution), (1, 2, 0, 3)))
    owns = [own_rows[:, at : at + step] for at, step in zip(starts, steps)]
    received = [from_others(own) for own in owns[:2]]
    source_rows = jnp.transpose(source, (1, 2, 0, 3))
    me = lax.axis_index("mode")
    first = (cond_count - me * cond_local) % cond_count
    info = jnp.stack([first, parity, me * local_modes, me * cond_local]).astype(jnp.int32)
    whole = pl.BlockSpec(memory_space=pltpu.VMEM)
    scalars = pl.BlockSpec(memory_space=pltpu.SMEM)
    params = pltpu.CompilerParams(vmem_limit_bytes=VMEM)
    matrix = pl.pallas_call(
        functools.partial(coupling_kernel, cond_count, all_modes, local_modes),
        out_shape=jax.ShapeDtypeStruct((cond_count * local_modes, 5 * all_modes), jnp.bfloat16),
        in_specs=[scalars, whole],
        out_specs=whole,
        compiler_params=params,
    )(info, jnp.transpose(triples))
    cond_beyond = lax.ppermute(cond_own[:, :1], "space", second_pairs)
    cond_others, cond_beyond, _ = lax.optimization_barrier(
        (tuple(from_others(cond_own)), cond_beyond, matrix)
    )

    def by_rows(*blocks):
        return jnp.transpose(jnp.concatenate(blocks, axis=0), (1, 2, 0, 3))

    cond_all = by_rows(cond_own, *cond_others)
    cond_high = lax.ppermute(cond_all[planes - 1 :], "space", first_pairs)
    cond_low = by_rows(
        cond_beyond,
        lax.ppermute(jnp.concatenate(cond_others, axis=0)[:, :1], "space", second_pairs),
    )
    cond = jnp.concatenate([cond_low, cond_all, cond_high], axis=0)
    cond = jnp.pad(cond, ((0, 0), (1, 1), (0, 0), (0, 0)))

    def across(*arrays):
        return lax.ppermute(jnp.concatenate(arrays, axis=0), "space", second_pairs)

    halo_own = across(lax.optimization_barrier((own_rows[0], cond_high))[0])
    edge_shape = jax.ShapeDtypeStruct((planes, local_modes, size_z), jnp.float32)
    mixed_scratch = pltpu.VMEM((SLOTS, cond_count * local_modes, size_z), jnp.float32)
    results, faces, pending = [], [], []
    reason = matrix
    for c, step in enumerate(steps):
        pieces, held, _ = lax.optimization_barrier((received[c], info, reason))
        total, face, edge_low, edge_high, scale = pl.pallas_call(
            functools.partial(apply_kernel, starts[c], cond_count, local_modes),
            out_shape=(
                jax.ShapeDtypeStruct((planes, step, local_modes, size_z), jnp.float32),
                jax.ShapeDtypeStruct((step, local_modes, size_z), jnp.float32),
                edge_shape,
                edge_shape,
                jax.ShapeDtypeStruct((planes, step, size_z), jnp.float32),
            ),
            in_specs=[scalars] + [whole] * 3 + [pl.BlockSpec(memory_space=pl.ANY)],
            out_specs=(whole,) * 5,
            scratch_shapes=[
                pltpu.VMEM((planes, step + 2, all_modes, size_z), jnp.bfloat16),
                pltpu.VMEM((planes, step, 2 * all_modes, size_z), jnp.bfloat16),
                pltpu.VMEM((size_z, size_z), jnp.bfloat16),
                pltpu.VMEM((planes + 2, step + 2, cond_count, size_z), jnp.bfloat16),
                pltpu.VMEM((planes + 2, step + 2, cond_count, size_z), jnp.float32),
                pltpu.VMEM((SLOTS, 4, cond_count, size_z), jnp.float32),
                mixed_scratch,
                mixed_scratch,
                pltpu.VMEM((planes, step, local_modes, size_z), jnp.float32),
                pltpu.SemaphoreType.DMA,
            ],
            compiler_params=params,
        )(held, matrix, owns[c], jnp.concatenate(pieces, axis=2), cond)
        reason = scale
        if c == 0:
            received += [from_others(lax.optimization_barrier((own, scale))[0]) for own in owns[2:]]
            pieces = lax.optimization_barrier((pieces, scale))[0]
        pending.append([piece[0] for piece in pieces])
        results += [total, edge_low, edge_high, scale, owns[c]]
        faces.append(face)

    halo_early = across(*pending[0], *pending[1])
    halo_late = across(*pending[2])
    faces, _, _, _ = lax.optimization_barrier((faces, halo_own, halo_early, halo_late))
    from_first = lax.ppermute(jnp.concatenate(faces, axis=0), "space", first_pairs)
    halves = size_z // LANES
    return pl.pallas_call(
        functools.partial(finish_kernel, steps, cond_count, local_modes),
        out_shape=jax.ShapeDtypeStruct((local_modes, planes, size_y, size_z), jnp.float32),
        in_specs=[scalars] + [whole] * (7 + len(results)),
        out_specs=pl.BlockSpec(memory_space=pl.ANY),
        scratch_shapes=[
            pltpu.VMEM((SLOTS, cond_count, size_z), jnp.float32),
            mixed_scratch,
            pltpu.SemaphoreType.DMA((2, halves)),
        ]
        + [pltpu.VMEM((local_modes, planes, BAND, LANES), jnp.float32)] * (2 * halves),
        compiler_params=params,
    )(info, matrix, cond, from_first, halo_own, halo_early, halo_late, source_rows, *results)


def solution(mesh):
    return jax.shard_map(
        shards,
        mesh=mesh,
        in_specs=(
            P("mode", "space", None, None),
            P("mode", "space", None, None),
            P("mode", "space", None, None),
            P(),
        ),
        out_specs=P("mode", "space", None, None),
        check_vma=False,
    )
```

```python
import functools

import jax
import jax.numpy as jnp
from jax import lax
from jax.experimental import pallas as pl
from jax.experimental.pallas import tpu as pltpu
from jax.sharding import PartitionSpec as P

UNITS = (5, 5, 6)
BAND = 8
SLOTS = 4
PARTS = 4
LANES = 128
VMEM = 18 * 2**20

weight_scale = 16.0
relax_factor = 2.0 / 3.0


def pairings(axis):
    count = lax.axis_size(axis)
    found = []
    for start in (0, 1):
        pairs = [(i, i + 1) for i in range(start, count - 1, 2)]
        found.append(pairs + [(high, low) for low, high in pairs])
    return found


def from_others(block):
    count = lax.axis_size("mode")
    return [
        lax.ppermute(block, "mode", [((i + step) % count, i) for i in range(count)])
        for step in range(1, count)
    ]


def coupling_kernel(cond_count, all_modes, local_modes, info, triples, matrix):
    inner = PARTS if cond_count % PARTS == 0 else 1
    entries = triples.shape[1]
    width = min(entries, 512)
    total = jnp.zeros((cond_count // inner * local_modes, inner * all_modes), jnp.float32)
    for start in range(0, entries, width):
        here = slice(start, start + width)
        row = triples[0:1, here] - info[2]
        column = triples[1:2, here] - info[2]
        column = jnp.where(column < 0, column + all_modes, column)
        mode = triples[2:3, here] - info[3]
        mode = jnp.where(mode < 0, mode + cond_count, mode)
        weight = triples[3:4, here].astype(jnp.float32)
        upper = mode // inner
        inside = (row >= 0) & (row < local_modes)
        left_code = jnp.where(inside, upper * local_modes + row, -1)
        right_code = (mode - upper * inner) * all_modes + column
        left = jnp.where(
            left_code == lax.broadcasted_iota(jnp.int32, (total.shape[0], width), 0), weight, 0.0
        )
        right = jnp.where(
            right_code == lax.broadcasted_iota(jnp.int32, (total.shape[1], width), 0), 1.0, 0.0
        )
        total = total + lax.dot_general(
            left.astype(jnp.bfloat16),
            right.astype(jnp.bfloat16),
            (((1,), (1,)), ((), ())),
            preferred_element_type=jnp.float32,
        )
    coupling = (total / weight_scale).astype(jnp.bfloat16).astype(jnp.float32) * 0.5
    for mode in range(cond_count):
        upper, lower = divmod(mode, inner)
        block = coupling[
            upper * local_modes : (upper + 1) * local_modes, lower * all_modes : (lower + 1) * all_modes
        ]
        wide = jnp.concatenate([block] + [-block] * 4, axis=1)
        matrix[mode * local_modes : (mode + 1) * local_modes, :] = wide.astype(jnp.bfloat16)


def apply_kernel(row0, cond_count, local_modes, info, matrix, own, other, cond_all, total, face, edge_low, edge_high, scale, field, summed, band, cond, plain, weights, mixed, around, product, sem):
    planes, rows, size_z = total.shape[0], total.shape[1], total.shape[3]
    all_modes = field.shape[2]
    slots = mixed.shape[0]
    steps = [(y, x) for y in range(rows) for x in range(planes)]
    window = pltpu.make_async_copy(cond_all.at[:, row0 : row0 + rows + 2], cond, sem)
    window.start()
    blank = jnp.zeros((planes, all_modes, size_z), jnp.bfloat16)
    field[:, 0] = blank
    field[:, rows + 1] = blank
    field[:, 1 : rows + 1, :local_modes, :] = own[...]
    field[:, 1 : rows + 1, local_modes:, :] = other[...]
    to = lax.broadcasted_iota(jnp.int32, (size_z, size_z), 0)
    at = lax.broadcasted_iota(jnp.int32, (size_z, size_z), 1)
    band[...] = jnp.where(jnp.abs(to - at) == 1, 1.0, 0.0).astype(jnp.bfloat16)
    window.wait()
    plain[...] = cond[...].astype(jnp.float32)
    lane = lax.broadcasted_iota(jnp.int32, (cond_count, size_z), 1)
    lane_out = lax.broadcasted_iota(jnp.int32, (local_modes, size_z), 1)

    def both_sides(value, lanes):
        above = jnp.where(lanes == size_z - 1, 0.0, pltpu.roll(value, size_z - 1, 1))
        below = jnp.where(lanes == 0, 0.0, pltpu.roll(value, 1, 1))
        return above + below

    def nearby_sum(y, x):
        value = jnp.dot(field[x, y + 1], band[...], preferred_element_type=jnp.float32)
        for side in (x - 1, x + 1):
            if 0 <= side < planes:
                value = value + field[side, y + 1].astype(jnp.float32)
        coarse = value.astype(jnp.bfloat16)
        summed[x, y, :all_modes] = coarse
        summed[x, y, all_modes:] = (value - coarse.astype(jnp.float32)).astype(jnp.bfloat16)

    def mix(step):
        y, x = steps[step]
        slot = step % slots
        mixed[slot] = jnp.dot(matrix[:, :all_modes], field[x, y + 1], preferred_element_type=jnp.float32)
        nearby = jnp.concatenate([summed[x, y], field[x, y], field[x, y + 2]], axis=0)
        around[slot] = jnp.dot(matrix[:, all_modes:], nearby, preferred_element_type=jnp.float32)

    def sums(step):
        y, x = steps[step]
        slot = step % slots
        centre = plain[x + 1, y + 1]
        low, high = plain[x, y + 1], plain[x + 2, y + 1]
        front, back = plain[x + 1, y], plain[x + 1, y + 2]
        weights[slot, 0] = 6.0 * centre + ((low + high) + (front + back)) + both_sides(centre, lane)
        outer = []
        if x == planes - 1:
            outer.append((high, face, (y,)))
        if y == 0:
            outer.append((front, edge_low, (x,)))
        if y == rows - 1:
            outer.append((back, edge_high, (x,)))
        for n, (side, _, _) in enumerate(outer):
            weights[slot, 1 + n] = centre + side
        scale[x, y : y + 1, :] = (2.0 * relax_factor) / weights[slot, 0, pl.ds(info[0], 1), :]
        for start in range(0, size_z, LANES):
            part = slice(start, start + LANES)
            accs = [None] * (2 + len(outer))

            def add(which, term):
                accs[which] = term if accs[which] is None else accs[which] + term

            for k in range(cond_count):
                here = slice(k * local_modes, (k + 1) * local_modes)
                value = mixed[slot, here, part]
                middle = jnp.broadcast_to(plain[x + 1, y + 1, k : k + 1, part], value.shape)
                add(1, middle * value)
                add(0, middle * around[slot, here, part])
                for n in range(1 + len(outer)):
                    weight = jnp.broadcast_to(weights[slot, n, k : k + 1, part], value.shape)
                    add(n + (n > 0), weight * value)
            total[x, y, :, part] = accs[0]
            product[x, y, :, part] = accs[1]
            for n, (_, target, index) in enumerate(outer):
                target[(*index, slice(None), part)] = accs[2 + n]

    def close(y):
        for x in range(planes):
            value = total[x, y] - both_sides(product[x, y], lane_out)
            for side in (x - 1, x + 1):
                if 0 <= side < planes:
                    value = value - product[side, y]
            for side in (y - 1, y + 1):
                if 0 <= side < rows:
                    value = value - product[x, side]
            total[x, y] = value

    ahead = slots - 1
    for step in range(len(steps)):
        nearby_sum(*steps[step])
    for step in range(ahead):
        mix(step)
    for step in range(len(steps)):
        if step + ahead < len(steps):
            mix(step + ahead)
        sums(step)
        y, x = steps[step]
        if x == planes - 1 and y > 0:
            close(y - 1)
    close(rows - 1)


def beyond_kernel(steps, cond_count, local_modes, info, matrix, cond, own, other, halo_own, halo_mid, halo_late, result, missing, weights, mixed):
    slots = mixed.shape[0]
    size_z = result.shape[2]
    places = [(c, y) for c in range(len(steps)) for y in range(steps[c])]
    total_rows = len(places)
    all_modes = matrix.shape[1] // 5
    pieces = all_modes // local_modes - 1
    tasks = []
    for row, (c, _) in enumerate(places):
        tasks += [(row, True), (row, False)] if c == 0 else [(row, False)]

    def planes_beyond(row):
        c, y = places[row]
        found = [halo_own[row]]
        for piece in range(pieces):
            if c < 2:
                found.append(halo_mid[pieces * sum(steps[:c]) + piece * steps[c] + y])
            else:
                found.append(halo_late[piece * steps[c] + y])
        return found

    def mix(task):
        row, inside = tasks[task]
        if inside:
            part, planes = slice(all_modes, 2 * all_modes), [own[0, row], other[0, row]]
        else:
            part, planes = slice(0, all_modes), planes_beyond(row)
        mixed[task % slots] = jnp.dot(
            matrix[:, part], jnp.concatenate(planes, axis=0), preferred_element_type=jnp.float32
        )

    for task in range(slots - 1):
        mix(task)
    for task, (row, inside) in enumerate(tasks):
        if task + slots - 1 < len(tasks):
            mix(task + slots - 1)
        slot = task % slots
        weight = cond[0, row + 1].astype(jnp.float32)
        weights[slot] = weight if inside else weight + cond[1, row + 1].astype(jnp.float32)
        if inside:
            mean = weights[slot, pl.ds(info[0], 1), :]
            missing[row : row + 1, :] = mean / (2.0 * relax_factor)
        for start in range(0, size_z, LANES):
            part = slice(start, start + LANES)
            acc = result[row, :, part] if places[row][0] == 0 and not inside else None
            for k in range(cond_count):
                value = mixed[slot, k * local_modes : (k + 1) * local_modes, part]
                term = jnp.broadcast_to(weights[slot, k : k + 1, part], value.shape) * value
                acc = term if acc is None else acc + term
            result[row, :, part] = acc


def finish_kernel(steps, info, from_high, from_low, missing, source, *rest):
    chunks = len(steps)
    per_chunk = [rest[5 * c : 5 * c + 5] for c in range(chunks)]
    result, sem = rest[5 * chunks], rest[5 * chunks + 1]
    planes, _, modes, size_z = per_chunk[0][0].shape
    halves = size_z // LANES
    stages = [rest[5 * chunks + 2 + slot * halves :][:halves] for slot in range(2)]
    parity = info[1]
    places = [(c, y) for c in range(chunks) for y in range(steps[c])]
    total_rows = len(places)
    copies = []
    for band in range(total_rows // BAND):
        stage = stages[band % 2]
        if band >= 2:
            for copy in copies[band - 2]:
                copy.wait()
        for line in range(BAND):
            row = band * BAND + line
            c, y = places[row]
            total, _, _, scale, own = per_chunk[c]
            for x in range(planes):
                natural = x + parity * (planes - 1 - 2 * x)
                applied = total[x, y]
                if x == 0:
                    applied = applied - from_low[row]
                if x == planes - 1:
                    applied = applied - from_high[row]
                if y == 0 and c > 0:
                    applied = applied - per_chunk[c - 1][2][x]
                if y == steps[c] - 1 and c < chunks - 1:
                    applied = applied - per_chunk[c + 1][1][x]
                factor = scale[x, y : y + 1, :]
                if c == 0 and x == 0:
                    factor = factor / (1.0 + factor * missing[y : y + 1, :])
                value = own[x, y].astype(jnp.float32) + (
                    source[natural, row].astype(jnp.float32) - applied
                ) * factor
                for h in range(halves):
                    flat = stage[h].reshape(modes * planes * BAND, LANES)
                    flat[pl.ds(natural * BAND + line, modes, planes * BAND), :] = value[
                        :, h * LANES : (h + 1) * LANES
                    ]
        copies.append(
            [
                pltpu.make_async_copy(
                    stage[h],
                    result.at[:, :, band * BAND : (band + 1) * BAND, h * LANES : (h + 1) * LANES],
                    sem.at[band % 2, h],
                )
                for h in range(halves)
            ]
        )
        for copy in copies[band]:
            copy.start()
    for waiting in copies[-2:]:
        for copy in waiting:
            copy.wait()


def shards(solution, source, conductivity, triples):
    mode_count = lax.axis_size("mode")
    local_modes, planes, size_y, size_z = solution.shape
    all_modes = local_modes * mode_count
    cond_local = conductivity.shape[0]
    cond_count = cond_local * mode_count
    first_pairs, second_pairs = pairings("space")
    unit = size_y // sum(UNITS)
    chunks = len(UNITS)
    starts = [unit * sum(UNITS[:c]) for c in range(chunks)]
    steps = [unit * units for units in UNITS]
    parity = lax.axis_index("space") % 2

    def oriented(block):
        return jnp.where(parity == 0, block, jnp.flip(block, 1))

    cond_own = oriented(conductivity)
    own_rows = lax.optimization_barrier(jnp.transpose(oriented(solution), (1, 2, 0, 3)))
    def across(*arrays):
        return lax.ppermute(jnp.concatenate(arrays, axis=0), "space", second_pairs)

    cond_edge = jnp.transpose(cond_own[:, 0], (1, 0, 2))
    mixture = across(own_rows[0].reshape(-1, size_z), cond_edge.reshape(-1, size_z))
    halo_own = mixture[: size_y * local_modes].reshape(size_y, local_modes, size_z)
    cond_beyond = mixture[size_y * local_modes :].reshape(size_y, cond_local, size_z)
    owns = [own_rows[:, at : at + step] for at, step in zip(starts, steps)]
    received = [from_others(owns[0])]
    me = lax.axis_index("mode")
    first = (cond_count - me * cond_local) % cond_count
    info = jnp.stack([first, parity, me * local_modes, me * cond_local]).astype(jnp.int32)
    whole = pl.BlockSpec(memory_space=pltpu.VMEM)
    scalars = pl.BlockSpec(memory_space=pltpu.SMEM)
    params = pltpu.CompilerParams(vmem_limit_bytes=VMEM)
    matrix = pl.pallas_call(
        functools.partial(coupling_kernel, cond_count, all_modes, local_modes),
        out_shape=jax.ShapeDtypeStruct((cond_count * local_modes, 5 * all_modes), jnp.bfloat16),
        in_specs=[scalars, whole],
        out_specs=whole,
        compiler_params=params,
    )(info, jnp.transpose(triples))
    cond_others, _ = lax.optimization_barrier((tuple(from_others(cond_own)), matrix))
    cond_all = jnp.transpose(jnp.concatenate([cond_own, *cond_others], axis=0), (1, 2, 0, 3))
    cond_high = lax.ppermute(cond_all[planes - 1 :], "space", first_pairs)
    cond_further = across(cond_all[0, :, cond_local:])

    def padded(low):
        rows = jnp.concatenate([low, cond_all, cond_high], axis=0)
        return jnp.pad(rows, ((0, 0), (1, 1), (0, 0), (0, 0)))

    cond = padded(jnp.zeros_like(cond_high))

    received.append(from_others(lax.optimization_barrier((owns[1], received[0]))[0]))
    edge_shape = jax.ShapeDtypeStruct((planes, local_modes, size_z), jnp.float32)
    mixed_scratch = pltpu.VMEM((SLOTS, cond_count * local_modes, size_z), jnp.float32)
    results, faces, pending = [], [], []
    reason = matrix
    for c, step in enumerate(steps):
        pieces, held, _ = lax.optimization_barrier((received[c], info, reason))
        total, face, edge_low, edge_high, scale = pl.pallas_call(
            functools.partial(apply_kernel, starts[c], cond_count, local_modes),
            out_shape=(
                jax.ShapeDtypeStruct((planes, step, local_modes, size_z), jnp.float32),
                jax.ShapeDtypeStruct((step, local_modes, size_z), jnp.float32),
                edge_shape,
                edge_shape,
                jax.ShapeDtypeStruct((planes, step, size_z), jnp.float32),
            ),
            in_specs=[scalars] + [whole] * 3 + [pl.BlockSpec(memory_space=pl.ANY)],
            out_specs=(whole,) * 5,
            scratch_shapes=[
                pltpu.VMEM((planes, step + 2, all_modes, size_z), jnp.bfloat16),
                pltpu.VMEM((planes, step, 2 * all_modes, size_z), jnp.bfloat16),
                pltpu.VMEM((size_z, size_z), jnp.bfloat16),
                pltpu.VMEM((planes + 2, step + 2, cond_count, size_z), jnp.bfloat16),
                pltpu.VMEM((planes + 2, step + 2, cond_count, size_z), jnp.float32),
                pltpu.VMEM((SLOTS, 4, cond_count, size_z), jnp.float32),
                mixed_scratch,
                mixed_scratch,
                pltpu.VMEM((planes, step, local_modes, size_z), jnp.float32),
                pltpu.SemaphoreType.DMA,
            ],
            compiler_params=params,
        )(held, matrix, owns[c], jnp.concatenate(pieces, axis=2), cond)
        reason = scale
        if c == 0:
            cond_low, _ = lax.optimization_barrier(((cond_beyond, cond_further), scale))
            cond_low = jnp.concatenate(cond_low, axis=1)
            cond = padded(cond_low[None])
            received += [from_others(lax.optimization_barrier((own, scale))[0]) for own in owns[2:]]
        pending.append([piece[0] for piece in pieces])
        results += [total, edge_low, edge_high, scale, owns[c]]
        faces.append(face)

    halo_mid = across(*pending[0], *pending[1])
    halo_late = across(*pending[2])
    source_rows = jnp.transpose(source, (1, 2, 0, 3))
    faces, _, _ = lax.optimization_barrier((faces, halo_mid, halo_late))
    from_high = lax.ppermute(jnp.concatenate(faces, axis=0), "space", first_pairs)
    from_low, missing = pl.pallas_call(
        functools.partial(beyond_kernel, steps, cond_count, local_modes),
        out_shape=(
            jax.ShapeDtypeStruct((size_y, local_modes, size_z), jnp.float32),
            jax.ShapeDtypeStruct((steps[0], size_z), jnp.float32),
        ),
        in_specs=[scalars] + [whole] * 7,
        out_specs=(whole,) * 2,
        scratch_shapes=[pltpu.VMEM((SLOTS, cond_count, size_z), jnp.float32), mixed_scratch],
        compiler_params=params,
    )(info, matrix, cond, owns[0], jnp.concatenate(received[0], axis=2), halo_own, halo_mid, halo_late)
    halves = size_z // LANES
    return pl.pallas_call(
        functools.partial(finish_kernel, steps),
        out_shape=jax.ShapeDtypeStruct((local_modes, planes, size_y, size_z), jnp.float32),
        in_specs=[scalars] + [whole] * (4 + len(results)),
        out_specs=pl.BlockSpec(memory_space=pl.ANY),
        scratch_shapes=[pltpu.SemaphoreType.DMA((2, halves))]
        + [pltpu.VMEM((local_modes, planes, BAND, LANES), jnp.float32)] * (2 * halves),
        compiler_params=params,
    )(info, from_high, from_low, missing, source_rows, *results)


def solution(mesh):
    return jax.shard_map(
        shards,
        mesh=mesh,
        in_specs=(
            P("mode", "space", None, None),
            P("mode", "space", None, None),
            P("mode", "space", None, None),
            P(),
        ),
        out_specs=P("mode", "space", None, None),
        check_vma=False,
    )
```

```python
import functools

import jax
import jax.numpy as jnp
from jax import lax
from jax.experimental import pallas as pl
from jax.experimental.pallas import tpu as pltpu
from jax.sharding import PartitionSpec as P

UNITS = (5, 5, 6)
BAND = 8
SLOTS = 4
PARTS = 4
LANES = 128
VMEM = 18 * 2**20

weight_scale = 16.0
relax_factor = 2.0 / 3.0


def pairings(axis):
    count = lax.axis_size(axis)
    found = []
    for start in (0, 1):
        pairs = [(i, i + 1) for i in range(start, count - 1, 2)]
        found.append(pairs + [(high, low) for low, high in pairs])
    return found


def from_others(block):
    count = lax.axis_size("mode")
    return [
        lax.ppermute(block, "mode", [((i + step) % count, i) for i in range(count)])
        for step in range(1, count)
    ]


def coupling_kernel(cond_count, all_modes, local_modes, info, triples, matrix):
    inner = PARTS if cond_count % PARTS == 0 else 1
    entries = triples.shape[1]
    width = min(entries, 512)
    total = jnp.zeros((cond_count // inner * local_modes, inner * all_modes), jnp.float32)
    for start in range(0, entries, width):
        here = slice(start, start + width)
        row = triples[0:1, here] - info[2]
        column = triples[1:2, here] - info[2]
        column = jnp.where(column < 0, column + all_modes, column)
        mode = triples[2:3, here] - info[3]
        mode = jnp.where(mode < 0, mode + cond_count, mode)
        weight = triples[3:4, here].astype(jnp.float32)
        upper = mode // inner
        inside = (row >= 0) & (row < local_modes)
        left_code = jnp.where(inside, upper * local_modes + row, -1)
        right_code = (mode - upper * inner) * all_modes + column
        left = jnp.where(
            left_code == lax.broadcasted_iota(jnp.int32, (total.shape[0], width), 0), weight, 0.0
        )
        right = jnp.where(
            right_code == lax.broadcasted_iota(jnp.int32, (total.shape[1], width), 0), 1.0, 0.0
        )
        total = total + lax.dot_general(
            left.astype(jnp.bfloat16),
            right.astype(jnp.bfloat16),
            (((1,), (1,)), ((), ())),
            preferred_element_type=jnp.float32,
        )
    coupling = (total / weight_scale).astype(jnp.bfloat16).astype(jnp.float32) * 0.5
    for mode in range(cond_count):
        upper, lower = divmod(mode, inner)
        block = coupling[
            upper * local_modes : (upper + 1) * local_modes, lower * all_modes : (lower + 1) * all_modes
        ]
        wide = jnp.concatenate([block] + [-block] * 4, axis=1)
        matrix[mode * local_modes : (mode + 1) * local_modes, :] = wide.astype(jnp.bfloat16)


def apply_kernel(row0, cond_count, local_modes, info, matrix, own, other, cond_all, total, face, edge_low, edge_high, scale, field, summed, band, cond, plain, weights, mixed, around, product, sem):
    planes, rows, size_z = total.shape[0], total.shape[1], total.shape[3]
    all_modes = field.shape[2]
    slots = mixed.shape[0]
    steps = [(y, x) for y in range(rows) for x in range(planes)]
    window = pltpu.make_async_copy(cond_all.at[:, row0 : row0 + rows + 2], cond, sem)
    window.start()
    blank = jnp.zeros((planes, all_modes, size_z), jnp.bfloat16)
    field[:, 0] = blank
    field[:, rows + 1] = blank
    field[:, 1 : rows + 1, :local_modes, :] = own[...]
    field[:, 1 : rows + 1, local_modes:, :] = other[...]
    to = lax.broadcasted_iota(jnp.int32, (size_z, size_z), 0)
    at = lax.broadcasted_iota(jnp.int32, (size_z, size_z), 1)
    band[...] = jnp.where(jnp.abs(to - at) == 1, 1.0, 0.0).astype(jnp.bfloat16)
    window.wait()
    plain[...] = cond[...].astype(jnp.float32)
    lane = lax.broadcasted_iota(jnp.int32, (cond_count, size_z), 1)
    lane_out = lax.broadcasted_iota(jnp.int32, (local_modes, size_z), 1)

    def both_sides(value, lanes):
        above = jnp.where(lanes == size_z - 1, 0.0, pltpu.roll(value, size_z - 1, 1))
        below = jnp.where(lanes == 0, 0.0, pltpu.roll(value, 1, 1))
        return above + below

    def nearby_sum(y, x):
        value = jnp.dot(field[x, y + 1], band[...], preferred_element_type=jnp.float32)
        for side in (x - 1, x + 1):
            if 0 <= side < planes:
                value = value + field[side, y + 1].astype(jnp.float32)
        coarse = value.astype(jnp.bfloat16)
        summed[x, y, :all_modes] = coarse
        summed[x, y, all_modes:] = (value - coarse.astype(jnp.float32)).astype(jnp.bfloat16)

    def mix(step):
        y, x = steps[step]
        slot = step % slots
        mixed[slot] = jnp.dot(matrix[:, :all_modes], field[x, y + 1], preferred_element_type=jnp.float32)
        nearby = jnp.concatenate([summed[x, y], field[x, y], field[x, y + 2]], axis=0)
        around[slot] = jnp.dot(matrix[:, all_modes:], nearby, preferred_element_type=jnp.float32)

    def sums(step):
        y, x = steps[step]
        slot = step % slots
        centre = plain[x + 1, y + 1]
        low, high = plain[x, y + 1], plain[x + 2, y + 1]
        front, back = plain[x + 1, y], plain[x + 1, y + 2]
        weights[slot, 0] = 6.0 * centre + ((low + high) + (front + back)) + both_sides(centre, lane)
        outer = []
        if x == planes - 1:
            outer.append((high, face, (y,)))
        if y == 0:
            outer.append((front, edge_low, (x,)))
        if y == rows - 1:
            outer.append((back, edge_high, (x,)))
        for n, (side, _, _) in enumerate(outer):
            weights[slot, 1 + n] = centre + side
        scale[x, y : y + 1, :] = (2.0 * relax_factor) / weights[slot, 0, pl.ds(info[0], 1), :]
        for start in range(0, size_z, LANES):
            part = slice(start, start + LANES)
            accs = [None] * (2 + len(outer))

            def add(which, term):
                accs[which] = term if accs[which] is None else accs[which] + term

            for k in range(cond_count):
                here = slice(k * local_modes, (k + 1) * local_modes)
                value = mixed[slot, here, part]
                middle = jnp.broadcast_to(plain[x + 1, y + 1, k : k + 1, part], value.shape)
                add(1, middle * value)
                add(0, middle * around[slot, here, part])
                for n in range(1 + len(outer)):
                    weight = jnp.broadcast_to(weights[slot, n, k : k + 1, part], value.shape)
                    add(n + (n > 0), weight * value)
            total[x, y, :, part] = accs[0]
            product[x, y, :, part] = accs[1]
            for n, (_, target, index) in enumerate(outer):
                target[(*index, slice(None), part)] = accs[2 + n]

    def close(y):
        for x in range(planes):
            value = total[x, y] - both_sides(product[x, y], lane_out)
            for side in (x - 1, x + 1):
                if 0 <= side < planes:
                    value = value - product[side, y]
            for side in (y - 1, y + 1):
                if 0 <= side < rows:
                    value = value - product[x, side]
            total[x, y] = value

    ahead = slots - 1
    for step in range(len(steps)):
        nearby_sum(*steps[step])
    for step in range(ahead):
        mix(step)
    for step in range(len(steps)):
        if step + ahead < len(steps):
            mix(step + ahead)
        sums(step)
        y, x = steps[step]
        if x == planes - 1 and y > 0:
            close(y - 1)
    close(rows - 1)


def beyond_kernel(steps, cond_count, local_modes, info, matrix, cond, own, other, halo_low, halo_mid, halo_late, result, missing, weights, mixed):
    slots = mixed.shape[0]
    size_z = result.shape[2]
    places = [(c, y) for c in range(len(steps)) for y in range(steps[c])]
    total_rows = len(places)
    all_modes = matrix.shape[1] // 5
    pieces = all_modes // local_modes - 1
    low_rows = halo_low.shape[0]
    high_rows = total_rows - low_rows
    tasks = []
    for row, (c, _) in enumerate(places):
        tasks += [(row, True), (row, False)] if c == 0 else [(row, False)]

    def planes_beyond(row):
        c, y = places[row]
        found = [halo_low[row] if row < low_rows else halo_mid[row - low_rows]]
        for piece in range(pieces):
            if c < 2:
                found.append(halo_mid[high_rows + pieces * sum(steps[:c]) + piece * steps[c] + y])
            else:
                found.append(halo_late[piece * steps[c] + y])
        return found

    def mix(task):
        row, inside = tasks[task]
        if inside:
            part, planes = slice(all_modes, 2 * all_modes), [own[0, row], other[0, row]]
        else:
            part, planes = slice(0, all_modes), planes_beyond(row)
        mixed[task % slots] = jnp.dot(
            matrix[:, part], jnp.concatenate(planes, axis=0), preferred_element_type=jnp.float32
        )

    for task in range(slots - 1):
        mix(task)
    for task, (row, inside) in enumerate(tasks):
        if task + slots - 1 < len(tasks):
            mix(task + slots - 1)
        slot = task % slots
        weight = cond[0, row + 1].astype(jnp.float32)
        weights[slot] = weight if inside else weight + cond[1, row + 1].astype(jnp.float32)
        if inside:
            mean = weights[slot, pl.ds(info[0], 1), :]
            missing[row : row + 1, :] = mean / (2.0 * relax_factor)
        for start in range(0, size_z, LANES):
            part = slice(start, start + LANES)
            acc = result[row, :, part] if places[row][0] == 0 and not inside else None
            for k in range(cond_count):
                value = mixed[slot, k * local_modes : (k + 1) * local_modes, part]
                term = jnp.broadcast_to(weights[slot, k : k + 1, part], value.shape) * value
                acc = term if acc is None else acc + term
            result[row, :, part] = acc


def finish_kernel(steps, info, from_high, from_low, missing, source, *rest):
    chunks = len(steps)
    per_chunk = [rest[5 * c : 5 * c + 5] for c in range(chunks)]
    result, sem = rest[5 * chunks], rest[5 * chunks + 1]
    planes, _, modes, size_z = per_chunk[0][0].shape
    halves = size_z // LANES
    stages = [rest[5 * chunks + 2 + slot * halves :][:halves] for slot in range(2)]
    parity = info[1]
    places = [(c, y) for c in range(chunks) for y in range(steps[c])]
    total_rows = len(places)
    copies = []
    for band in range(total_rows // BAND):
        stage = stages[band % 2]
        if band >= 2:
            for copy in copies[band - 2]:
                copy.wait()
        for line in range(BAND):
            row = band * BAND + line
            c, y = places[row]
            total, _, _, scale, own = per_chunk[c]
            for x in range(planes):
                natural = x + parity * (planes - 1 - 2 * x)
                applied = total[x, y]
                if x == 0:
                    applied = applied - from_low[row]
                if x == planes - 1:
                    applied = applied - from_high[row]
                if y == 0 and c > 0:
                    applied = applied - per_chunk[c - 1][2][x]
                if y == steps[c] - 1 and c < chunks - 1:
                    applied = applied - per_chunk[c + 1][1][x]
                factor = scale[x, y : y + 1, :]
                if c == 0 and x == 0:
                    factor = factor / (1.0 + factor * missing[y : y + 1, :])
                value = own[x, y].astype(jnp.float32) + (
                    source[natural, row].astype(jnp.float32) - applied
                ) * factor
                for h in range(halves):
                    flat = stage[h].reshape(modes * planes * BAND, LANES)
                    flat[pl.ds(natural * BAND + line, modes, planes * BAND), :] = value[
                        :, h * LANES : (h + 1) * LANES
                    ]
        copies.append(
            [
                pltpu.make_async_copy(
                    stage[h],
                    result.at[:, :, band * BAND : (band + 1) * BAND, h * LANES : (h + 1) * LANES],
                    sem.at[band % 2, h],
                )
                for h in range(halves)
            ]
        )
        for copy in copies[band]:
            copy.start()
    for waiting in copies[-2:]:
        for copy in waiting:
            copy.wait()


def shards(solution, source, conductivity, triples):
    mode_count = lax.axis_size("mode")
    local_modes, planes, size_y, size_z = solution.shape
    all_modes = local_modes * mode_count
    cond_local = conductivity.shape[0]
    cond_count = cond_local * mode_count
    first_pairs, second_pairs = pairings("space")
    unit = size_y // sum(UNITS)
    chunks = len(UNITS)
    starts = [unit * sum(UNITS[:c]) for c in range(chunks)]
    steps = [unit * units for units in UNITS]
    parity = lax.axis_index("space") % 2

    def oriented(block):
        return jnp.where(parity == 0, block, jnp.flip(block, 1))

    cond_own = oriented(conductivity)
    own_rows = lax.optimization_barrier(jnp.transpose(oriented(solution), (1, 2, 0, 3)))
    half = 3 * size_y // 4

    def across(*arrays):
        return lax.ppermute(jnp.concatenate(arrays, axis=0), "space", second_pairs)

    cond_edge = jnp.transpose(cond_own[:, 0], (1, 0, 2))
    mixture = across(own_rows[0, :half].reshape(-1, size_z), cond_edge.reshape(-1, size_z))
    halo_low = mixture[: half * local_modes].reshape(half, local_modes, size_z)
    cond_beyond = mixture[half * local_modes :].reshape(size_y, cond_local, size_z)
    owns = [own_rows[:, at : at + step] for at, step in zip(starts, steps)]
    received = [from_others(owns[0])]
    me = lax.axis_index("mode")
    first = (cond_count - me * cond_local) % cond_count
    info = jnp.stack([first, parity, me * local_modes, me * cond_local]).astype(jnp.int32)
    whole = pl.BlockSpec(memory_space=pltpu.VMEM)
    scalars = pl.BlockSpec(memory_space=pltpu.SMEM)
    params = pltpu.CompilerParams(vmem_limit_bytes=VMEM)
    matrix = pl.pallas_call(
        functools.partial(coupling_kernel, cond_count, all_modes, local_modes),
        out_shape=jax.ShapeDtypeStruct((cond_count * local_modes, 5 * all_modes), jnp.bfloat16),
        in_specs=[scalars, whole],
        out_specs=whole,
        compiler_params=params,
    )(info, jnp.transpose(triples))
    cond_others, _ = lax.optimization_barrier((tuple(from_others(cond_own)), matrix))
    cond_all = jnp.transpose(jnp.concatenate([cond_own, *cond_others], axis=0), (1, 2, 0, 3))
    cond_high = lax.ppermute(cond_all[planes - 1 :], "space", first_pairs)
    cond_further = across(cond_all[0, :, cond_local:])

    def padded(low):
        rows = jnp.concatenate([low, cond_all, cond_high], axis=0)
        return jnp.pad(rows, ((0, 0), (1, 1), (0, 0), (0, 0)))

    cond = padded(jnp.zeros_like(cond_high))

    received.append(from_others(lax.optimization_barrier((owns[1], received[0]))[0]))
    edge_shape = jax.ShapeDtypeStruct((planes, local_modes, size_z), jnp.float32)
    mixed_scratch = pltpu.VMEM((SLOTS, cond_count * local_modes, size_z), jnp.float32)
    results, faces, pending = [], [], []
    reason = matrix
    for c, step in enumerate(steps):
        pieces, held, _ = lax.optimization_barrier((received[c], info, reason))
        total, face, edge_low, edge_high, scale = pl.pallas_call(
            functools.partial(apply_kernel, starts[c], cond_count, local_modes),
            out_shape=(
                jax.ShapeDtypeStruct((planes, step, local_modes, size_z), jnp.float32),
                jax.ShapeDtypeStruct((step, local_modes, size_z), jnp.float32),
                edge_shape,
                edge_shape,
                jax.ShapeDtypeStruct((planes, step, size_z), jnp.float32),
            ),
            in_specs=[scalars] + [whole] * 3 + [pl.BlockSpec(memory_space=pl.ANY)],
            out_specs=(whole,) * 5,
            scratch_shapes=[
                pltpu.VMEM((planes, step + 2, all_modes, size_z), jnp.bfloat16),
                pltpu.VMEM((planes, step, 2 * all_modes, size_z), jnp.bfloat16),
                pltpu.VMEM((size_z, size_z), jnp.bfloat16),
                pltpu.VMEM((planes + 2, step + 2, cond_count, size_z), jnp.bfloat16),
                pltpu.VMEM((planes + 2, step + 2, cond_count, size_z), jnp.float32),
                pltpu.VMEM((SLOTS, 4, cond_count, size_z), jnp.float32),
                mixed_scratch,
                mixed_scratch,
                pltpu.VMEM((planes, step, local_modes, size_z), jnp.float32),
                pltpu.SemaphoreType.DMA,
            ],
            compiler_params=params,
        )(held, matrix, owns[c], jnp.concatenate(pieces, axis=2), cond)
        reason = scale
        if c == 0:
            cond_low, _ = lax.optimization_barrier(((cond_beyond, cond_further), scale))
            cond_low = jnp.concatenate(cond_low, axis=1)
            cond = padded(cond_low[None])
            received += [from_others(lax.optimization_barrier((own, scale))[0]) for own in owns[2:]]
        pending.append([piece[0] for piece in pieces])
        results += [total, edge_low, edge_high, scale, owns[c]]
        faces.append(face)

    halo_mid = across(own_rows[0, half:], *pending[0], *pending[1])
    halo_late = across(*pending[2])
    source_rows = jnp.transpose(source, (1, 2, 0, 3))
    faces, _, _ = lax.optimization_barrier((faces, halo_mid, halo_late))
    from_high = lax.ppermute(jnp.concatenate(faces, axis=0), "space", first_pairs)
    from_low, missing = pl.pallas_call(
        functools.partial(beyond_kernel, steps, cond_count, local_modes),
        out_shape=(
            jax.ShapeDtypeStruct((size_y, local_modes, size_z), jnp.float32),
            jax.ShapeDtypeStruct((steps[0], size_z), jnp.float32),
        ),
        in_specs=[scalars] + [whole] * 7,
        out_specs=(whole,) * 2,
        scratch_shapes=[pltpu.VMEM((SLOTS, cond_count, size_z), jnp.float32), mixed_scratch],
        compiler_params=params,
    )(info, matrix, cond, owns[0], jnp.concatenate(received[0], axis=2), halo_low, halo_mid, halo_late)
    halves = size_z // LANES
    return pl.pallas_call(
        functools.partial(finish_kernel, steps),
        out_shape=jax.ShapeDtypeStruct((local_modes, planes, size_y, size_z), jnp.float32),
        in_specs=[scalars] + [whole] * (4 + len(results)),
        out_specs=pl.BlockSpec(memory_space=pl.ANY),
        scratch_shapes=[pltpu.SemaphoreType.DMA((2, halves))]
        + [pltpu.VMEM((local_modes, planes, BAND, LANES), jnp.float32)] * (2 * halves),
        compiler_params=params,
    )(info, from_high, from_low, missing, source_rows, *results)


def solution(mesh):
    return jax.shard_map(
        shards,
        mesh=mesh,
        in_specs=(
            P("mode", "space", None, None),
            P("mode", "space", None, None),
            P("mode", "space", None, None),
            P(),
        ),
        out_specs=P("mode", "space", None, None),
        check_vma=False,
    )
```

```python
import functools

import jax
import jax.numpy as jnp
from jax import lax
from jax.experimental import pallas as pl
from jax.experimental.pallas import tpu as pltpu
from jax.sharding import PartitionSpec as P

UNITS = (5, 5, 6)
BAND = 8
SLOTS = 4
PARTS = 4
LANES = 128
VMEM = 18 * 2**20

weight_scale = 16.0
relax_factor = 2.0 / 3.0


def pairings(axis):
    count = lax.axis_size(axis)
    found = []
    for start in (0, 1):
        pairs = [(i, i + 1) for i in range(start, count - 1, 2)]
        found.append(pairs + [(high, low) for low, high in pairs])
    return found


def from_others(block):
    count = lax.axis_size("mode")
    return [
        lax.ppermute(block, "mode", [((i + step) % count, i) for i in range(count)])
        for step in range(1, count)
    ]


def coupling_kernel(cond_count, all_modes, local_modes, info, triples, matrix):
    inner = PARTS if cond_count % PARTS == 0 else 1
    entries = triples.shape[1]
    width = min(entries, 512)
    total = jnp.zeros((cond_count // inner * local_modes, inner * all_modes), jnp.float32)
    for start in range(0, entries, width):
        here = slice(start, start + width)
        row = triples[0:1, here] - info[2]
        column = triples[1:2, here] - info[2]
        column = jnp.where(column < 0, column + all_modes, column)
        mode = triples[2:3, here] - info[3]
        mode = jnp.where(mode < 0, mode + cond_count, mode)
        weight = triples[3:4, here].astype(jnp.float32)
        upper = mode // inner
        inside = (row >= 0) & (row < local_modes)
        left_code = jnp.where(inside, upper * local_modes + row, -1)
        right_code = (mode - upper * inner) * all_modes + column
        left = jnp.where(
            left_code == lax.broadcasted_iota(jnp.int32, (total.shape[0], width), 0), weight, 0.0
        )
        right = jnp.where(
            right_code == lax.broadcasted_iota(jnp.int32, (total.shape[1], width), 0), 1.0, 0.0
        )
        total = total + lax.dot_general(
            left.astype(jnp.bfloat16),
            right.astype(jnp.bfloat16),
            (((1,), (1,)), ((), ())),
            preferred_element_type=jnp.float32,
        )
    coupling = (total / weight_scale).astype(jnp.bfloat16).astype(jnp.float32) * 0.5
    for mode in range(cond_count):
        upper, lower = divmod(mode, inner)
        block = coupling[
            upper * local_modes : (upper + 1) * local_modes, lower * all_modes : (lower + 1) * all_modes
        ]
        wide = jnp.concatenate([block] + [-block] * 4, axis=1)
        matrix[mode * local_modes : (mode + 1) * local_modes, :] = wide.astype(jnp.bfloat16)


def apply_kernel(row0, cond_count, local_modes, info, matrix, own, other, cond_all, total, face, edge_low, edge_high, scale, field, summed, band, cond, plain, weights, mixed, around, product, sem):
    planes, rows, size_z = total.shape[0], total.shape[1], total.shape[3]
    all_modes = field.shape[2]
    slots = mixed.shape[0]
    steps = [(y, x) for y in range(rows) for x in range(planes)]
    window = pltpu.make_async_copy(cond_all.at[:, row0 : row0 + rows + 2], cond, sem)
    window.start()
    blank = jnp.zeros((planes, all_modes, size_z), jnp.bfloat16)
    field[:, 0] = blank
    field[:, rows + 1] = blank
    field[:, 1 : rows + 1, :local_modes, :] = own[...]
    field[:, 1 : rows + 1, local_modes:, :] = other[...]
    to = lax.broadcasted_iota(jnp.int32, (size_z, size_z), 0)
    at = lax.broadcasted_iota(jnp.int32, (size_z, size_z), 1)
    band[...] = jnp.where(jnp.abs(to - at) == 1, 1.0, 0.0).astype(jnp.bfloat16)
    window.wait()
    plain[...] = cond[...].astype(jnp.float32)
    lane = lax.broadcasted_iota(jnp.int32, (cond_count, size_z), 1)
    lane_out = lax.broadcasted_iota(jnp.int32, (local_modes, size_z), 1)

    def both_sides(value, lanes):
        above = jnp.where(lanes == size_z - 1, 0.0, pltpu.roll(value, size_z - 1, 1))
        below = jnp.where(lanes == 0, 0.0, pltpu.roll(value, 1, 1))
        return above + below

    def nearby_sum(y, x):
        value = jnp.dot(field[x, y + 1], band[...], preferred_element_type=jnp.float32)
        for side in (x - 1, x + 1):
            if 0 <= side < planes:
                value = value + field[side, y + 1].astype(jnp.float32)
        value = value + (field[x, y].astype(jnp.float32) + field[x, y + 2].astype(jnp.float32))
        coarse = value.astype(jnp.bfloat16)
        summed[x, y, :all_modes] = coarse
        summed[x, y, all_modes:] = (value - coarse.astype(jnp.float32)).astype(jnp.bfloat16)

    def mix(step):
        y, x = steps[step]
        slot = step % slots
        mixed[slot] = jnp.dot(matrix[:, :all_modes], field[x, y + 1], preferred_element_type=jnp.float32)
        around[slot] = jnp.dot(
            matrix[:, all_modes : 3 * all_modes], summed[x, y], preferred_element_type=jnp.float32
        )

    def sums(step):
        y, x = steps[step]
        slot = step % slots
        centre = plain[x + 1, y + 1]
        low, high = plain[x, y + 1], plain[x + 2, y + 1]
        front, back = plain[x + 1, y], plain[x + 1, y + 2]
        weights[slot, 0] = 6.0 * centre + ((low + high) + (front + back)) + both_sides(centre, lane)
        outer = []
        if x == planes - 1:
            outer.append((high, face, (y,)))
        if y == 0:
            outer.append((front, edge_low, (x,)))
        if y == rows - 1:
            outer.append((back, edge_high, (x,)))
        for n, (side, _, _) in enumerate(outer):
            weights[slot, 1 + n] = centre + side
        scale[x, y : y + 1, :] = (2.0 * relax_factor) / weights[slot, 0, pl.ds(info[0], 1), :]
        for start in range(0, size_z, LANES):
            part = slice(start, start + LANES)
            accs = [None] * (2 + len(outer))

            def add(which, term):
                accs[which] = term if accs[which] is None else accs[which] + term

            for k in range(cond_count):
                here = slice(k * local_modes, (k + 1) * local_modes)
                value = mixed[slot, here, part]
                middle = jnp.broadcast_to(plain[x + 1, y + 1, k : k + 1, part], value.shape)
                add(1, middle * value)
                add(0, middle * around[slot, here, part])
                for n in range(1 + len(outer)):
                    weight = jnp.broadcast_to(weights[slot, n, k : k + 1, part], value.shape)
                    add(n + (n > 0), weight * value)
            total[x, y, :, part] = accs[0]
            product[x, y, :, part] = accs[1]
            for n, (_, target, index) in enumerate(outer):
                target[(*index, slice(None), part)] = accs[2 + n]

    def close(y):
        for x in range(planes):
            value = total[x, y] - both_sides(product[x, y], lane_out)
            for side in (x - 1, x + 1):
                if 0 <= side < planes:
                    value = value - product[side, y]
            for side in (y - 1, y + 1):
                if 0 <= side < rows:
                    value = value - product[x, side]
            total[x, y] = value

    ahead = slots - 1
    for step in range(len(steps)):
        nearby_sum(*steps[step])
    for step in range(ahead):
        mix(step)
    for step in range(len(steps)):
        if step + ahead < len(steps):
            mix(step + ahead)
        sums(step)
        y, x = steps[step]
        if x == planes - 1 and y > 0:
            close(y - 1)
    close(rows - 1)


def beyond_kernel(steps, cond_count, local_modes, info, matrix, cond, own, other, halo_low, halo_mid, halo_late, result, missing, weights, mixed):
    slots = mixed.shape[0]
    size_z = result.shape[2]
    places = [(c, y) for c in range(len(steps)) for y in range(steps[c])]
    total_rows = len(places)
    all_modes = matrix.shape[1] // 5
    pieces = all_modes // local_modes - 1
    low_rows = halo_low.shape[0]
    high_rows = total_rows - low_rows
    tasks = []
    for row, (c, _) in enumerate(places):
        tasks += [(row, True), (row, False)] if c == 0 else [(row, False)]

    def planes_beyond(row):
        c, y = places[row]
        found = [halo_low[row] if row < low_rows else halo_mid[row - low_rows]]
        for piece in range(pieces):
            if c < 2:
                found.append(halo_mid[high_rows + pieces * sum(steps[:c]) + piece * steps[c] + y])
            else:
                found.append(halo_late[piece * steps[c] + y])
        return found

    def mix(task):
        row, inside = tasks[task]
        if inside:
            part, planes = slice(all_modes, 2 * all_modes), [own[0, row], other[0, row]]
        else:
            part, planes = slice(0, all_modes), planes_beyond(row)
        mixed[task % slots] = jnp.dot(
            matrix[:, part], jnp.concatenate(planes, axis=0), preferred_element_type=jnp.float32
        )

    for task in range(slots - 1):
        mix(task)
    for task, (row, inside) in enumerate(tasks):
        if task + slots - 1 < len(tasks):
            mix(task + slots - 1)
        slot = task % slots
        weight = cond[0, row + 1].astype(jnp.float32)
        weights[slot] = weight if inside else weight + cond[1, row + 1].astype(jnp.float32)
        if inside:
            mean = weights[slot, pl.ds(info[0], 1), :]
            missing[row : row + 1, :] = mean / (2.0 * relax_factor)
        for start in range(0, size_z, LANES):
            part = slice(start, start + LANES)
            acc = result[row, :, part] if places[row][0] == 0 and not inside else None
            for k in range(cond_count):
                value = mixed[slot, k * local_modes : (k + 1) * local_modes, part]
                term = jnp.broadcast_to(weights[slot, k : k + 1, part], value.shape) * value
                acc = term if acc is None else acc + term
            result[row, :, part] = acc


def finish_kernel(steps, info, from_high, from_low, missing, source, *rest):
    chunks = len(steps)
    per_chunk = [rest[5 * c : 5 * c + 5] for c in range(chunks)]
    result, sem = rest[5 * chunks], rest[5 * chunks + 1]
    planes, _, modes, size_z = per_chunk[0][0].shape
    halves = size_z // LANES
    stages = [rest[5 * chunks + 2 + slot * halves :][:halves] for slot in range(2)]
    parity = info[1]
    places = [(c, y) for c in range(chunks) for y in range(steps[c])]
    total_rows = len(places)
    copies = []
    for band in range(total_rows // BAND):
        stage = stages[band % 2]
        if band >= 2:
            for copy in copies[band - 2]:
                copy.wait()
        for line in range(BAND):
            row = band * BAND + line
            c, y = places[row]
            total, _, _, scale, own = per_chunk[c]
            for x in range(planes):
                natural = x + parity * (planes - 1 - 2 * x)
                applied = total[x, y]
                if x == 0:
                    applied = applied - from_low[row]
                if x == planes - 1:
                    applied = applied - from_high[row]
                if y == 0 and c > 0:
                    applied = applied - per_chunk[c - 1][2][x]
                if y == steps[c] - 1 and c < chunks - 1:
                    applied = applied - per_chunk[c + 1][1][x]
                factor = scale[x, y : y + 1, :]
                if c == 0 and x == 0:
                    factor = factor / (1.0 + factor * missing[y : y + 1, :])
                value = own[x, y].astype(jnp.float32) + (
                    source[natural, row].astype(jnp.float32) - applied
                ) * factor
                for h in range(halves):
                    flat = stage[h].reshape(modes * planes * BAND, LANES)
                    flat[pl.ds(natural * BAND + line, modes, planes * BAND), :] = value[
                        :, h * LANES : (h + 1) * LANES
                    ]
        copies.append(
            [
                pltpu.make_async_copy(
                    stage[h],
                    result.at[:, :, band * BAND : (band + 1) * BAND, h * LANES : (h + 1) * LANES],
                    sem.at[band % 2, h],
                )
                for h in range(halves)
            ]
        )
        for copy in copies[band]:
            copy.start()
    for waiting in copies[-2:]:
        for copy in waiting:
            copy.wait()


def shards(solution, source, conductivity, triples):
    mode_count = lax.axis_size("mode")
    local_modes, planes, size_y, size_z = solution.shape
    all_modes = local_modes * mode_count
    cond_local = conductivity.shape[0]
    cond_count = cond_local * mode_count
    first_pairs, second_pairs = pairings("space")
    unit = size_y // sum(UNITS)
    chunks = len(UNITS)
    starts = [unit * sum(UNITS[:c]) for c in range(chunks)]
    steps = [unit * units for units in UNITS]
    parity = lax.axis_index("space") % 2

    def oriented(block):
        return jnp.where(parity == 0, block, jnp.flip(block, 1))

    cond_own = oriented(conductivity)
    own_rows = lax.optimization_barrier(jnp.transpose(oriented(solution), (1, 2, 0, 3)))
    half = 3 * size_y // 4

    def across(*arrays):
        return lax.ppermute(jnp.concatenate(arrays, axis=0), "space", second_pairs)

    cond_edge = jnp.transpose(cond_own[:, 0], (1, 0, 2))
    mixture = across(own_rows[0, :half].reshape(-1, size_z), cond_edge.reshape(-1, size_z))
    halo_low = mixture[: half * local_modes].reshape(half, local_modes, size_z)
    cond_beyond = mixture[half * local_modes :].reshape(size_y, cond_local, size_z)
    owns = [own_rows[:, at : at + step] for at, step in zip(starts, steps)]
    received = [from_others(owns[0])]
    me = lax.axis_index("mode")
    first = (cond_count - me * cond_local) % cond_count
    info = jnp.stack([first, parity, me * local_modes, me * cond_local]).astype(jnp.int32)
    whole = pl.BlockSpec(memory_space=pltpu.VMEM)
    scalars = pl.BlockSpec(memory_space=pltpu.SMEM)
    params = pltpu.CompilerParams(vmem_limit_bytes=VMEM)
    matrix = pl.pallas_call(
        functools.partial(coupling_kernel, cond_count, all_modes, local_modes),
        out_shape=jax.ShapeDtypeStruct((cond_count * local_modes, 5 * all_modes), jnp.bfloat16),
        in_specs=[scalars, whole],
        out_specs=whole,
        compiler_params=params,
    )(info, jnp.transpose(triples))
    cond_others, _ = lax.optimization_barrier((tuple(from_others(cond_own)), matrix))
    cond_all = jnp.transpose(jnp.concatenate([cond_own, *cond_others], axis=0), (1, 2, 0, 3))
    cond_high = lax.ppermute(cond_all[planes - 1 :], "space", first_pairs)
    cond_further = across(cond_all[0, :, cond_local:])

    def padded(low):
        rows = jnp.concatenate([low, cond_all, cond_high], axis=0)
        return jnp.pad(rows, ((0, 0), (1, 1), (0, 0), (0, 0)))

    cond = padded(jnp.zeros_like(cond_high))

    received.append(from_others(lax.optimization_barrier((owns[1], received[0]))[0]))
    edge_shape = jax.ShapeDtypeStruct((planes, local_modes, size_z), jnp.float32)
    mixed_scratch = pltpu.VMEM((SLOTS, cond_count * local_modes, size_z), jnp.float32)
    results, faces, pending = [], [], []
    source_rows = jnp.transpose(source, (1, 2, 0, 3))
    reason = (matrix, source_rows)
    for c, step in enumerate(steps):
        pieces, held, _ = lax.optimization_barrier((received[c], info, reason))
        total, face, edge_low, edge_high, scale = pl.pallas_call(
            functools.partial(apply_kernel, starts[c], cond_count, local_modes),
            out_shape=(
                jax.ShapeDtypeStruct((planes, step, local_modes, size_z), jnp.float32),
                jax.ShapeDtypeStruct((step, local_modes, size_z), jnp.float32),
                edge_shape,
                edge_shape,
                jax.ShapeDtypeStruct((planes, step, size_z), jnp.float32),
            ),
            in_specs=[scalars] + [whole] * 3 + [pl.BlockSpec(memory_space=pl.ANY)],
            out_specs=(whole,) * 5,
            scratch_shapes=[
                pltpu.VMEM((planes, step + 2, all_modes, size_z), jnp.bfloat16),
                pltpu.VMEM((planes, step, 2 * all_modes, size_z), jnp.bfloat16),
                pltpu.VMEM((size_z, size_z), jnp.bfloat16),
                pltpu.VMEM((planes + 2, step + 2, cond_count, size_z), jnp.bfloat16),
                pltpu.VMEM((planes + 2, step + 2, cond_count, size_z), jnp.float32),
                pltpu.VMEM((SLOTS, 4, cond_count, size_z), jnp.float32),
                mixed_scratch,
                mixed_scratch,
                pltpu.VMEM((planes, step, local_modes, size_z), jnp.float32),
                pltpu.SemaphoreType.DMA,
            ],
            compiler_params=params,
        )(held, matrix, owns[c], jnp.concatenate(pieces, axis=2), cond)
        reason = scale
        if c == 0:
            cond_low, _ = lax.optimization_barrier(((cond_beyond, cond_further), scale))
            cond_low = jnp.concatenate(cond_low, axis=1)
            cond = padded(cond_low[None])
            received += [from_others(lax.optimization_barrier((own, scale))[0]) for own in owns[2:]]
        pending.append([piece[0] for piece in pieces])
        results += [total, edge_low, edge_high, scale, owns[c]]
        faces.append(face)

    halo_mid = across(own_rows[0, half:], *pending[0], *pending[1])
    halo_late = across(*pending[2])
    faces, _, _ = lax.optimization_barrier((faces, halo_mid, halo_late))
    from_high = lax.ppermute(jnp.concatenate(faces, axis=0), "space", first_pairs)
    from_low, missing = pl.pallas_call(
        functools.partial(beyond_kernel, steps, cond_count, local_modes),
        out_shape=(
            jax.ShapeDtypeStruct((size_y, local_modes, size_z), jnp.float32),
            jax.ShapeDtypeStruct((steps[0], size_z), jnp.float32),
        ),
        in_specs=[scalars] + [whole] * 7,
        out_specs=(whole,) * 2,
        scratch_shapes=[pltpu.VMEM((SLOTS, cond_count, size_z), jnp.float32), mixed_scratch],
        compiler_params=params,
    )(info, matrix, cond, owns[0], jnp.concatenate(received[0], axis=2), halo_low, halo_mid, halo_late)
    halves = size_z // LANES
    return pl.pallas_call(
        functools.partial(finish_kernel, steps),
        out_shape=jax.ShapeDtypeStruct((local_modes, planes, size_y, size_z), jnp.float32),
        in_specs=[scalars] + [whole] * (4 + len(results)),
        out_specs=pl.BlockSpec(memory_space=pl.ANY),
        scratch_shapes=[pltpu.SemaphoreType.DMA((2, halves))]
        + [pltpu.VMEM((local_modes, planes, BAND, LANES), jnp.float32)] * (2 * halves),
        compiler_params=params,
    )(info, from_high, from_low, missing, source_rows, *results)


def solution(mesh):
    return jax.shard_map(
        shards,
        mesh=mesh,
        in_specs=(
            P("mode", "space", None, None),
            P("mode", "space", None, None),
            P("mode", "space", None, None),
            P(),
        ),
        out_specs=P("mode", "space", None, None),
        check_vma=False,
    )
```

```python
import functools

import jax
import jax.numpy as jnp
from jax import lax
from jax.experimental import pallas as pl
from jax.experimental.pallas import tpu as pltpu
from jax.sharding import PartitionSpec as P

UNITS = (5, 5, 6)
BAND = 8
SLOTS = 4
PARTS = 4
LANES = 128
VMEM = 18 * 2**20

weight_scale = 16.0
relax_factor = 2.0 / 3.0


def pairings(axis):
    count = lax.axis_size(axis)
    found = []
    for start in (0, 1):
        pairs = [(i, i + 1) for i in range(start, count - 1, 2)]
        found.append(pairs + [(high, low) for low, high in pairs])
    return found


def from_others(block):
    count = lax.axis_size("mode")
    return [
        lax.ppermute(block, "mode", [((i + step) % count, i) for i in range(count)])
        for step in range(1, count)
    ]


def coupling_kernel(cond_count, all_modes, local_modes, info, triples, matrix):
    inner = PARTS if cond_count % PARTS == 0 else 1
    entries = triples.shape[1]
    width = min(entries, 512)
    total = jnp.zeros((cond_count // inner * local_modes, inner * all_modes), jnp.float32)
    for start in range(0, entries, width):
        here = slice(start, start + width)
        row = triples[0:1, here] - info[2]
        column = triples[1:2, here] - info[2]
        column = jnp.where(column < 0, column + all_modes, column)
        mode = triples[2:3, here] - info[3]
        mode = jnp.where(mode < 0, mode + cond_count, mode)
        weight = triples[3:4, here].astype(jnp.float32)
        upper = mode // inner
        inside = (row >= 0) & (row < local_modes)
        left_code = jnp.where(inside, upper * local_modes + row, -1)
        right_code = (mode - upper * inner) * all_modes + column
        left = jnp.where(
            left_code == lax.broadcasted_iota(jnp.int32, (total.shape[0], width), 0), weight, 0.0
        )
        right = jnp.where(
            right_code == lax.broadcasted_iota(jnp.int32, (total.shape[1], width), 0), 1.0, 0.0
        )
        total = total + lax.dot_general(
            left.astype(jnp.bfloat16),
            right.astype(jnp.bfloat16),
            (((1,), (1,)), ((), ())),
            preferred_element_type=jnp.float32,
        )
    coupling = (total / weight_scale).astype(jnp.bfloat16).astype(jnp.float32) * 0.5
    for mode in range(cond_count):
        upper, lower = divmod(mode, inner)
        block = coupling[
            upper * local_modes : (upper + 1) * local_modes, lower * all_modes : (lower + 1) * all_modes
        ]
        wide = jnp.concatenate([block] + [-block] * 4, axis=1)
        matrix[mode * local_modes : (mode + 1) * local_modes, :] = wide.astype(jnp.bfloat16)


def apply_kernel(row0, cond_count, local_modes, info, matrix, own, other, cond_all, total, face, edge_low, edge_high, scale, field, summed, band, cond, plain, weights, mixed, around, product, sem):
    planes, rows, size_z = total.shape[0], total.shape[1], total.shape[3]
    all_modes = field.shape[2]
    slots = mixed.shape[0]
    steps = [(y, x) for y in range(rows) for x in range(planes)]
    window = pltpu.make_async_copy(cond_all.at[:, row0 : row0 + rows + 2], cond, sem)
    window.start()
    blank = jnp.zeros((planes, all_modes, size_z), jnp.bfloat16)
    field[:, 0] = blank
    field[:, rows + 1] = blank
    field[:, 1 : rows + 1, :local_modes, :] = own[...]
    field[:, 1 : rows + 1, local_modes:, :] = other[...]
    to = lax.broadcasted_iota(jnp.int32, (size_z, size_z), 0)
    at = lax.broadcasted_iota(jnp.int32, (size_z, size_z), 1)
    band[...] = jnp.where(jnp.abs(to - at) == 1, 1.0, 0.0).astype(jnp.bfloat16)
    window.wait()
    plain[...] = cond[...].astype(jnp.float32)
    lane = lax.broadcasted_iota(jnp.int32, (cond_count, size_z), 1)
    lane_out = lax.broadcasted_iota(jnp.int32, (local_modes, size_z), 1)

    def both_sides(value, lanes):
        above = jnp.where(lanes == size_z - 1, 0.0, pltpu.roll(value, size_z - 1, 1))
        below = jnp.where(lanes == 0, 0.0, pltpu.roll(value, 1, 1))
        return above + below

    def nearby_sum(y, x):
        value = jnp.dot(field[x, y + 1], band[...], preferred_element_type=jnp.float32)
        for side in (x - 1, x + 1):
            if 0 <= side < planes:
                value = value + field[side, y + 1].astype(jnp.float32)
        value = value + (field[x, y].astype(jnp.float32) + field[x, y + 2].astype(jnp.float32))
        coarse = value.astype(jnp.bfloat16)
        summed[x, y, :all_modes] = coarse
        summed[x, y, all_modes:] = (value - coarse.astype(jnp.float32)).astype(jnp.bfloat16)

    def mix(step):
        y, x = steps[step]
        slot = step % slots
        mixed[slot] = jnp.dot(matrix[:, :all_modes], field[x, y + 1], preferred_element_type=jnp.float32)
        around[slot] = jnp.dot(
            matrix[:, all_modes : 3 * all_modes], summed[x, y], preferred_element_type=jnp.float32
        )

    def sums(step):
        y, x = steps[step]
        slot = step % slots
        centre = plain[x + 1, y + 1]
        low, high = plain[x, y + 1], plain[x + 2, y + 1]
        front, back = plain[x + 1, y], plain[x + 1, y + 2]
        weights[slot, 0] = 6.0 * centre + ((low + high) + (front + back)) + both_sides(centre, lane)
        outer = []
        if x == planes - 1:
            outer.append((high, face, (y,)))
        if y == 0:
            outer.append((front, edge_low, (x,)))
        if y == rows - 1:
            outer.append((back, edge_high, (x,)))
        for n, (side, _, _) in enumerate(outer):
            weights[slot, 1 + n] = centre + side
        scale[x, y : y + 1, :] = (2.0 * relax_factor) / weights[slot, 0, pl.ds(info[0], 1), :]
        for start in range(0, size_z, LANES):
            part = slice(start, start + LANES)
            accs = [None] * (2 + len(outer))

            def add(which, term):
                accs[which] = term if accs[which] is None else accs[which] + term

            for k in range(cond_count):
                here = slice(k * local_modes, (k + 1) * local_modes)
                value = mixed[slot, here, part]
                middle = jnp.broadcast_to(plain[x + 1, y + 1, k : k + 1, part], value.shape)
                add(1, middle * value)
                add(0, middle * around[slot, here, part])
                for n in range(1 + len(outer)):
                    weight = jnp.broadcast_to(weights[slot, n, k : k + 1, part], value.shape)
                    add(n + (n > 0), weight * value)
            total[x, y, :, part] = accs[0]
            product[x, y, :, part] = accs[1]
            for n, (_, target, index) in enumerate(outer):
                target[(*index, slice(None), part)] = accs[2 + n]

    def close(y):
        for x in range(planes):
            value = total[x, y] - both_sides(product[x, y], lane_out)
            for side in (x - 1, x + 1):
                if 0 <= side < planes:
                    value = value - product[side, y]
            for side in (y - 1, y + 1):
                if 0 <= side < rows:
                    value = value - product[x, side]
            total[x, y] = value

    ahead = slots - 1
    for step in range(len(steps)):
        nearby_sum(*steps[step])
    for step in range(ahead):
        mix(step)
    for step in range(len(steps)):
        if step + ahead < len(steps):
            mix(step + ahead)
        sums(step)
        y, x = steps[step]
        if x == planes - 1 and y > 0:
            close(y - 1)
    close(rows - 1)


def beyond_kernel(steps, cond_count, local_modes, info, matrix, cond, own, other, halo_low, halo_mid, halo_late, result, missing, weights, mixed):
    slots = mixed.shape[0]
    size_z = result.shape[2]
    places = [(c, y) for c in range(len(steps)) for y in range(steps[c])]
    total_rows = len(places)
    all_modes = matrix.shape[1] // 5
    pieces = all_modes // local_modes - 1
    low_rows = halo_low.shape[0]
    high_rows = total_rows - low_rows
    tasks = []
    for row, (c, _) in enumerate(places):
        tasks += [(row, True), (row, False)] if c == 0 else [(row, False)]

    def planes_beyond(row):
        c, y = places[row]
        found = [halo_low[row] if row < low_rows else halo_mid[row - low_rows]]
        for piece in range(pieces):
            if c < 2:
                found.append(halo_mid[high_rows + pieces * sum(steps[:c]) + piece * steps[c] + y])
            else:
                found.append(halo_late[piece * steps[c] + y])
        return found

    def mix(task):
        row, inside = tasks[task]
        if inside:
            part, planes = slice(all_modes, 2 * all_modes), [own[0, row], other[0, row]]
        else:
            part, planes = slice(0, all_modes), planes_beyond(row)
        mixed[task % slots] = jnp.dot(
            matrix[:, part], jnp.concatenate(planes, axis=0), preferred_element_type=jnp.float32
        )

    for task in range(slots - 1):
        mix(task)
    for task, (row, inside) in enumerate(tasks):
        if task + slots - 1 < len(tasks):
            mix(task + slots - 1)
        slot = task % slots
        weight = cond[0, row + 1].astype(jnp.float32)
        weights[slot] = weight if inside else weight + cond[1, row + 1].astype(jnp.float32)
        if inside:
            mean = weights[slot, pl.ds(info[0], 1), :]
            missing[row : row + 1, :] = mean / (2.0 * relax_factor)
        for start in range(0, size_z, LANES):
            part = slice(start, start + LANES)
            acc = result[row, :, part] if places[row][0] == 0 and not inside else None
            for k in range(cond_count):
                value = mixed[slot, k * local_modes : (k + 1) * local_modes, part]
                term = jnp.broadcast_to(weights[slot, k : k + 1, part], value.shape) * value
                acc = term if acc is None else acc + term
            result[row, :, part] = acc


def finish_kernel(steps, info, from_high, from_low, missing, source, *rest):
    chunks = len(steps)
    per_chunk = [rest[5 * c : 5 * c + 5] for c in range(chunks)]
    result, sem = rest[5 * chunks], rest[5 * chunks + 1]
    planes, _, modes, size_z = per_chunk[0][0].shape
    halves = size_z // LANES
    stages = [rest[5 * chunks + 2 + slot * halves :][:halves] for slot in range(2)]
    parity = info[1]
    places = [(c, y) for c in range(chunks) for y in range(steps[c])]
    total_rows = len(places)
    copies = []
    for band in range(total_rows // BAND):
        stage = stages[band % 2]
        if band >= 2:
            for copy in copies[band - 2]:
                copy.wait()
        for line in range(BAND):
            row = band * BAND + line
            c, y = places[row]
            total, _, _, scale, own = per_chunk[c]
            for x in range(planes):
                natural = x + parity * (planes - 1 - 2 * x)
                applied = total[x, y]
                if x == 0:
                    applied = applied - from_low[row]
                if x == planes - 1:
                    applied = applied - from_high[row]
                if y == 0 and c > 0:
                    applied = applied - per_chunk[c - 1][2][x]
                if y == steps[c] - 1 and c < chunks - 1:
                    applied = applied - per_chunk[c + 1][1][x]
                factor = scale[x, y : y + 1, :]
                if c == 0 and x == 0:
                    factor = factor / (1.0 + factor * missing[y : y + 1, :])
                value = own[x, y].astype(jnp.float32) + (
                    source[natural, row].astype(jnp.float32) - applied
                ) * factor
                for h in range(halves):
                    flat = stage[h].reshape((modes + 1) * planes * BAND, LANES)
                    flat[pl.ds(natural * BAND + line, modes, planes * BAND), :] = value[
                        :, h * LANES : (h + 1) * LANES
                    ]
        copies.append(
            [
                pltpu.make_async_copy(
                    stage[h].at[:modes],
                    result.at[:, :, band * BAND : (band + 1) * BAND, h * LANES : (h + 1) * LANES],
                    sem.at[band % 2, h],
                )
                for h in range(halves)
            ]
        )
        for copy in copies[band]:
            copy.start()
    for waiting in copies[-2:]:
        for copy in waiting:
            copy.wait()


def shards(solution, source, conductivity, triples):
    mode_count = lax.axis_size("mode")
    local_modes, planes, size_y, size_z = solution.shape
    all_modes = local_modes * mode_count
    cond_local = conductivity.shape[0]
    cond_count = cond_local * mode_count
    first_pairs, second_pairs = pairings("space")
    unit = size_y // sum(UNITS)
    chunks = len(UNITS)
    starts = [unit * sum(UNITS[:c]) for c in range(chunks)]
    steps = [unit * units for units in UNITS]
    parity = lax.axis_index("space") % 2

    def oriented(block):
        return jnp.where(parity == 0, block, jnp.flip(block, 1))

    cond_own = oriented(conductivity)
    own_rows = lax.optimization_barrier(jnp.transpose(oriented(solution), (1, 2, 0, 3)))
    half = 3 * size_y // 4

    def across(*arrays):
        return lax.ppermute(jnp.concatenate(arrays, axis=0), "space", second_pairs)

    cond_edge = jnp.transpose(cond_own[:, 0], (1, 0, 2))
    mixture = across(own_rows[0, :half].reshape(-1, size_z), cond_edge.reshape(-1, size_z))
    halo_low = mixture[: half * local_modes].reshape(half, local_modes, size_z)
    cond_beyond = mixture[half * local_modes :].reshape(size_y, cond_local, size_z)
    owns = [own_rows[:, at : at + step] for at, step in zip(starts, steps)]
    received = [from_others(owns[0])]
    me = lax.axis_index("mode")
    first = (cond_count - me * cond_local) % cond_count
    info = jnp.stack([first, parity, me * local_modes, me * cond_local]).astype(jnp.int32)
    whole = pl.BlockSpec(memory_space=pltpu.VMEM)
    scalars = pl.BlockSpec(memory_space=pltpu.SMEM)
    params = pltpu.CompilerParams(vmem_limit_bytes=VMEM)
    matrix = pl.pallas_call(
        functools.partial(coupling_kernel, cond_count, all_modes, local_modes),
        out_shape=jax.ShapeDtypeStruct((cond_count * local_modes, 5 * all_modes), jnp.bfloat16),
        in_specs=[scalars, whole],
        out_specs=whole,
        compiler_params=params,
    )(info, jnp.transpose(triples))
    cond_others, _ = lax.optimization_barrier((tuple(from_others(cond_own)), matrix))
    cond_all = jnp.transpose(jnp.concatenate([cond_own, *cond_others], axis=0), (1, 2, 0, 3))
    cond_high = lax.ppermute(cond_all[planes - 1 :], "space", first_pairs)
    cond_further = across(cond_all[0, :, cond_local:])

    def padded(low):
        rows = jnp.concatenate([low, cond_all, cond_high], axis=0)
        return jnp.pad(rows, ((0, 0), (1, 1), (0, 0), (0, 0)))

    cond = padded(jnp.zeros_like(cond_high))

    received.append(from_others(lax.optimization_barrier((owns[1], received[0]))[0]))
    edge_shape = jax.ShapeDtypeStruct((planes, local_modes, size_z), jnp.float32)
    mixed_scratch = pltpu.VMEM((SLOTS, cond_count * local_modes, size_z), jnp.float32)
    results, faces, pending = [], [], []
    source_rows = jnp.transpose(source, (1, 2, 0, 3))
    reason = (matrix, source_rows)
    for c, step in enumerate(steps):
        pieces, held, _ = lax.optimization_barrier((received[c], info, reason))
        total, face, edge_low, edge_high, scale = pl.pallas_call(
            functools.partial(apply_kernel, starts[c], cond_count, local_modes),
            out_shape=(
                jax.ShapeDtypeStruct((planes, step, local_modes, size_z), jnp.float32),
                jax.ShapeDtypeStruct((step, local_modes, size_z), jnp.float32),
                edge_shape,
                edge_shape,
                jax.ShapeDtypeStruct((planes, step, size_z), jnp.float32),
            ),
            in_specs=[scalars] + [whole] * 3 + [pl.BlockSpec(memory_space=pl.ANY)],
            out_specs=(whole,) * 5,
            scratch_shapes=[
                pltpu.VMEM((planes, step + 2, all_modes, size_z), jnp.bfloat16),
                pltpu.VMEM((planes, step, 2 * all_modes, size_z), jnp.bfloat16),
                pltpu.VMEM((size_z, size_z), jnp.bfloat16),
                pltpu.VMEM((planes + 2, step + 2, cond_count, size_z), jnp.bfloat16),
                pltpu.VMEM((planes + 2, step + 2, cond_count, size_z), jnp.float32),
                pltpu.VMEM((SLOTS, 4, cond_count, size_z), jnp.float32),
                mixed_scratch,
                mixed_scratch,
                pltpu.VMEM((planes, step, local_modes, size_z), jnp.float32),
                pltpu.SemaphoreType.DMA,
            ],
            compiler_params=params,
        )(held, matrix, owns[c], jnp.concatenate(pieces, axis=2), cond)
        reason = scale
        if c == 0:
            cond_low, _ = lax.optimization_barrier(((cond_beyond, cond_further), scale))
            cond_low = jnp.concatenate(cond_low, axis=1)
            cond = padded(cond_low[None])
            received += [from_others(lax.optimization_barrier((own, scale))[0]) for own in owns[2:]]
        pending.append([piece[0] for piece in pieces])
        results += [total, edge_low, edge_high, scale, owns[c]]
        faces.append(face)

    halo_mid = across(own_rows[0, half:], *pending[0], *pending[1])
    halo_late = across(*pending[2])
    faces, _, _ = lax.optimization_barrier((faces, halo_mid, halo_late))
    from_high = lax.ppermute(jnp.concatenate(faces, axis=0), "space", first_pairs)
    from_low, missing = pl.pallas_call(
        functools.partial(beyond_kernel, steps, cond_count, local_modes),
        out_shape=(
            jax.ShapeDtypeStruct((size_y, local_modes, size_z), jnp.float32),
            jax.ShapeDtypeStruct((steps[0], size_z), jnp.float32),
        ),
        in_specs=[scalars] + [whole] * 7,
        out_specs=(whole,) * 2,
        scratch_shapes=[pltpu.VMEM((SLOTS, cond_count, size_z), jnp.float32), mixed_scratch],
        compiler_params=params,
    )(info, matrix, cond, owns[0], jnp.concatenate(received[0], axis=2), halo_low, halo_mid, halo_late)
    halves = size_z // LANES
    return pl.pallas_call(
        functools.partial(finish_kernel, steps),
        out_shape=jax.ShapeDtypeStruct((local_modes, planes, size_y, size_z), jnp.float32),
        in_specs=[scalars] + [whole] * (4 + len(results)),
        out_specs=pl.BlockSpec(memory_space=pl.ANY),
        scratch_shapes=[pltpu.SemaphoreType.DMA((2, halves))]
        + [pltpu.VMEM((local_modes + 1, planes, BAND, LANES), jnp.float32)] * (2 * halves),
        compiler_params=params,
    )(info, from_high, from_low, missing, source_rows, *results)


def solution(mesh):
    return jax.shard_map(
        shards,
        mesh=mesh,
        in_specs=(
            P("mode", "space", None, None),
            P("mode", "space", None, None),
            P("mode", "space", None, None),
            P(),
        ),
        out_specs=P("mode", "space", None, None),
        check_vma=False,
    )
```
